256 devices in a mesh: sta: 64 (over z_hi, y, x), freq: 4 (over z_lo, core).
Axes of the slice: x: 4, y: 4, z: 8 (z_hi: 4, z_lo: 2; z = z_hi * 2 + z_lo), core: 2. Of those that a mesh axis runs over, the one named last changes fastest.
Arguments:
- waveforms: bfloat16 [256, 4, 8192], P('sta'), may hold values from -6 to 6
- fir_taps: float32 [256, 256], P('sta'), may hold values from -0.375 to 0.375
- water_level: float32 [256], P('sta'), may hold values from 0.1 to 1
- gap_start: int32 [256, 4], P('sta'), may hold values from 0 to 8191
- gap_length: int32 [256, 4], P('sta'), may hold values from 0 to 2048
- live_slots: int32 [64], P('sta'), may hold values from 2 to 4, as said below
Outputs:
- correlations: bfloat16 [2, 96, 256, 4, 128], P(None, 'freq', 'sta')
The draws below stay inside these ranges and needn't reach their ends.
Inputs may be any that keep to these rules, and one draw needn't show every extreme that they name: Block d holds stations in its first live_slots[d] slots; the other slots are empty.
All inputs are finite; a program needn't handle non-finite values.
Results may differ from the reference program's by a relative error of at most 0.018.
Values may be sent and summed in bfloat16 or wider, within the bound.
A program may use at most 192 MiB of HBM per device.

```python
import math
import jax
import jax.numpy as jnp
from jax import lax

ROOT = 128
SEGLEN = 8192
TAPS = 256
LAGROWS = 96
SLOTS = 4
SEG = 4
ROUNDS = 2
STATIONS = 256
N_STA = 64


def draw_live_slots(key, part):
    key = jax.random.fold_in(key, 11)
    subkeys = jax.random.split(key, 3)
    counts = jax.random.randint(subkeys[0], (N_STA,), SLOTS // 2, SLOTS + 1)
    fullest = jax.random.randint(subkeys[1], (), 0, N_STA)
    emptiest = (fullest + 1 + jax.random.randint(subkeys[2], (), 0, N_STA - 1)) % N_STA
    counts = counts.at[fullest].set(SLOTS)
    counts = counts.at[emptiest].set(SLOTS // 2)
    return counts.astype(jnp.int32)


def set_ends(result, stream_key, least, high):
    longest = result.shape.index(max(result.shape))
    spots = []
    for shift in (0, 1):
        where = [jax.random.randint(jax.random.fold_in(stream_key, axis), (), 0, length) for axis, length in enumerate(result.shape)]
        where[longest] = (where[longest] + shift) % result.shape[longest]
        spots.append(tuple(where))
    return result.at[spots[0]].set(least).at[spots[1]].set(high)


def block_scale(stream_key, shape, cuts, smallest, top_value):
    loudness = 1.0
    for axis_at, shards_of in cuts:
        heights = jax.random.uniform(jax.random.fold_in(jax.random.fold_in(stream_key, 6), axis_at), (shards_of,), jnp.float32, smallest / len(cuts), top_value / len(cuts))
        loudness = loudness * jnp.repeat(jnp.exp(heights), shape[axis_at] // shards_of).reshape((-1,) + (1,) * (len(shape) - 1 - axis_at))
    return loudness


def noise(key, extent, scale, reach, cuts=(), kind=jnp.bfloat16):
    entries = scale * jax.random.normal(key, extent, jnp.float32)
    if cuts:
        entries = entries * block_scale(key, extent, cuts, -0.22, 0.18)
    return jnp.clip(entries, -reach, reach).astype(kind)


def setup_inputs(seed: int = 0) -> dict:
    key_list = jax.random.split(jax.random.key(seed), 7)
    waveforms = noise(key_list[0], (STATIONS, SEG, SEGLEN), 1.0, 6.0, ((0, 64),))
    fir_taps = noise(key_list[1], (STATIONS, TAPS), TAPS ** -0.5, 0.375, ((0, 64),), jnp.float32)
    water_level = jnp.clip(jnp.exp(math.log(1.0) - 2.3025851 * jax.random.uniform(key_list[2], (STATIONS,), jnp.float32) ** block_scale(key_list[2], (STATIONS,), ((0, 64),), -0.2, 0.2)), 0.1, 1.0)
    gap_start = set_ends(jax.random.randint(key_list[3], (STATIONS, SEG), 0, SEGLEN), jax.random.fold_in(key_list[3], 1), 0, SEGLEN - 1).astype(jnp.int32)
    gap_length = set_ends(jax.random.randint(key_list[4], (STATIONS, SEG), 0, SEGLEN // 4 + 1), jax.random.fold_in(key_list[4], 1), 0, (SEGLEN // 4 + 1) - 1).astype(jnp.int32)
    live_slots = draw_live_slots(jax.random.fold_in(key_list[6], 71), 0)
    return dict(waveforms=waveforms, fir_taps=fir_taps, water_level=water_level, gap_start=gap_start, gap_length=gap_length, live_slots=live_slots)


def station_spectra(inputs):
    record_raw, fir_row, water_row, start_row, length_row, alive_one = inputs
    samples = jnp.arange(SEGLEN, dtype=jnp.int32)[None, :]
    is_valid = (samples < start_row[:, None]) | (samples >= start_row[:, None] + length_row[:, None])
    record = jnp.where(is_valid, record_raw.astype(jnp.float32), jnp.zeros((), jnp.float32))
    spectrum = jnp.fft.fft(record, n=ROOT * ROOT, axis=-1) / jnp.sqrt(jnp.asarray(SEGLEN, jnp.float32))
    response = jnp.fft.fft(fir_row, n=ROOT * ROOT)
    whitened = response[None, :] * spectrum
    power_sum = jnp.real(whitened) ** 2 + jnp.imag(whitened) ** 2
    factor = alive_one / jnp.sqrt(power_sum + water_row)
    return ((jnp.real(whitened) * factor).astype(jnp.bfloat16), (jnp.imag(whitened) * factor).astype(jnp.bfloat16))

def reference(waveforms, fir_taps, water_level, gap_start, gap_length, live_slots):
    owners = jnp.arange(STATIONS, dtype=jnp.int32) // SLOTS
    places = jnp.arange(STATIONS, dtype=jnp.int32) % SLOTS
    alive_flag = (places < live_slots[owners]).astype(jnp.float32)
    norm_re, norm_im = lax.map(station_spectra, (waveforms, fir_taps, water_level, gap_start, gap_length, alive_flag))
    stride = N_STA // (2 * ROUNDS)
    lag_index = (jnp.arange(LAGROWS, dtype=jnp.int32) - LAGROWS // 2) % ROOT
    lag_scale = ROOT * ROOT / (SEG * ROOT * ROOT) ** 0.5

    def one_block(block_id):
        first = (block_id * SLOTS).astype(jnp.int32)
        own_re = lax.dynamic_slice_in_dim(norm_re, first, SLOTS, 0).astype(jnp.float32)
        own_im = lax.dynamic_slice_in_dim(norm_im, first, SLOTS, 0).astype(jnp.float32)
        results = []
        for round_index in range(ROUNDS):
            partner = ((block_id - (round_index + 1) * stride) % N_STA).astype(jnp.int32)
            far_re = lax.dynamic_slice_in_dim(norm_re, partner * SLOTS, SLOTS, 0).astype(jnp.float32)
            far_im = lax.dynamic_slice_in_dim(norm_im, partner * SLOTS, SLOTS, 0).astype(jnp.float32)
            cross_re = jnp.einsum('isk,jsk->ijk', own_re, far_re) + jnp.einsum('isk,jsk->ijk', own_im, far_im)
            cross_im = jnp.einsum('isk,jsk->ijk', own_im, far_re) - jnp.einsum('isk,jsk->ijk', own_re, far_im)
            lagged = jnp.real(jnp.fft.ifft(cross_re + 1j * cross_im, axis=-1)) * lag_scale
            lagged = lagged.reshape(SLOTS, SLOTS, ROOT, ROOT)[:, :, lag_index, :]
            results.append(jnp.transpose(lagged, (2, 0, 1, 3)).astype(jnp.bfloat16))
        return jnp.stack(results)
    blocks = lax.map(one_block, jnp.arange(N_STA, dtype=jnp.int32))
    return jnp.transpose(blocks, (1, 2, 0, 3, 4, 5)).reshape(ROUNDS, LAGROWS, STATIONS, SLOTS, ROOT)
```

```python
import functools
import math

import jax
import jax.numpy as jnp
import ml_dtypes
import numpy as np
from jax import lax
from jax.experimental import pallas as pl
from jax.experimental.pallas import tpu as pltpu
from jax.sharding import PartitionSpec as P

ROOT = 128
COARSE = 64
LAGROWS = 96
ROUNDS = 2
SLOTS = 4
SEG = 4
KEPT = 72
BAND = LAGROWS // 4
MESH = pl.DeviceIdType.MESH


def as_bf16(table):
    return table.astype(np.float32).astype(ml_dtypes.bfloat16)


def split_bf16(table):
    upper = as_bf16(table)
    return upper, as_bf16(table - upper.astype(np.float64))


def make_tables():
    kept = np.arange(KEPT)
    live = (kept <= 64).astype(np.float64)[:, None]
    full = np.arange(ROOT)
    angle = 2.0 * math.pi / ROOT
    first = kept[:, None] * np.arange(COARSE)[None, :] * angle
    first = np.concatenate([np.cos(first) * live, -np.sin(first) * live], axis=0)
    first_hi, first_lo = split_bf16(first)
    first_table = np.concatenate([first_hi, first_lo], axis=1)
    twist = kept[:, None] * full[None, :] * (angle / ROOT)
    weight = np.where((kept == 0) | (kept == 64), 1.0, 2.0)[:, None] * live
    weight = weight / math.sqrt(SEG * ROOT * ROOT)
    step = np.broadcast_to(kept[:, None] * angle, (KEPT, ROOT))
    twiddles = np.stack(
        [np.cos(twist), np.sin(twist), np.cos(twist) * weight, np.sin(twist) * weight, np.cos(step), np.sin(step)]
    ).astype(np.float32)
    square = full[:, None] * full[None, :] * angle
    cos_b, sin_b = np.cos(square), np.sin(square)
    last = np.block([[cos_b, -sin_b], [sin_b, cos_b]])
    last_hi, last_lo = split_bf16(last)
    inner = as_bf16(np.block([[cos_b, sin_b], [-sin_b, cos_b]]))
    square_tables = np.stack([last_hi, last_lo, inner])
    lag = (np.arange(LAGROWS) - LAGROWS // 2)[:, None] * kept[None, :] * angle
    outer = as_bf16(np.concatenate([np.cos(lag), -np.sin(lag)], axis=1))
    return first_table, twiddles, square_tables, outer


def dot(left, right):
    return jnp.dot(left, right, preferred_element_type=jnp.float32)


def spectra(wave, about, first_table, twiddles, squares):
    place = (
        lax.broadcasted_iota(jnp.int32, (COARSE, ROOT), 0) * ROOT
        + lax.broadcasted_iota(jnp.int32, (COARSE, ROOT), 1)
    ).astype(jnp.float32)
    records = []
    for s in range(SEG):
        start = about[4 + s : 5 + s, :]
        end = about[8 + s : 9 + s, :]
        gone = (place >= start) & (place < end)
        record = jnp.where(gone, 0.0, wave[s].astype(jnp.float32))
        records.append(record.astype(jnp.bfloat16))
    record = jnp.concatenate(records, axis=1)
    section = dot(first_table, jnp.concatenate([record, record], axis=0))
    cos_t, sin_t = twiddles[0], twiddles[1]
    tap0 = about[0:1, :]
    tap1 = about[1:2, :]
    rows = [(tap0 + tap1 * twiddles[4], -(tap1 * twiddles[5]))]
    for s in range(SEG):
        columns = section[:, s * ROOT : (s + 1) * ROOT]
        rows.append((columns[:KEPT], columns[KEPT:]))
    twisted = jnp.concatenate(
        [
            jnp.concatenate([re * cos_t + im * sin_t, im * cos_t - re * sin_t], axis=1)
            for re, im in rows
        ],
        axis=0,
    )
    upper = twisted.astype(jnp.bfloat16)
    lower = (twisted - upper.astype(jnp.float32)).astype(jnp.bfloat16)
    bins = dot(upper, squares[0]) + dot(lower, squares[0]) + dot(upper, squares[1])
    resp_re, resp_im = bins[:KEPT, :ROOT], bins[:KEPT, ROOT:]
    water = about[2:3, :]
    alive = about[3:4, :]
    found = []
    for s in range(SEG):
        part = bins[(s + 1) * KEPT : (s + 2) * KEPT]
        spec_re, spec_im = part[:, :ROOT], part[:, ROOT:]
        white_re = resp_re * spec_re - resp_im * spec_im
        white_im = resp_re * spec_im + resp_im * spec_re
        factor = alive * lax.rsqrt(white_re * white_re + white_im * white_im + water)
        found.append((white_re * factor, white_im * factor))
    return found


def kernel(
    n_sta,
    wave_ref,
    taps_ref,
    water_ref,
    start_ref,
    length_ref,
    live_ref,
    first_ref,
    twiddle_ref,
    square_ref,
    outer_ref,
    out_ref,
    about_ref,
    far_wave_ref,
    far_about_ref,
    own_ref,
    part_ref,
    got_ref,
    rows_ref,
    send_sem,
    recv_sem,
    part_send_sem,
    part_recv_sem,
):
    sta = lax.axis_index("sta")
    freq = lax.axis_index("freq")
    core = lax.rem(freq, 2)
    upper_chip = freq // 2
    stride = n_sta // (2 * ROUNDS)

    def block(steps):
        return lax.rem(sta + (steps % 4) * stride, n_sta)

    barrier = pltpu.get_barrier_semaphore()
    pl.semaphore_signal(barrier, inc=1, device_id={"sta": block(-1), "freq": 2 + core}, device_id_type=MESH)
    pl.semaphore_signal(
        barrier,
        inc=1,
        device_id={"sta": block(-2), "freq": 2 * (1 - upper_chip) + core},
        device_id_type=MESH,
    )
    for step in range(1, 4):
        pl.semaphore_signal(
            barrier, inc=1, device_id={"sta": sta, "freq": lax.rem(freq + step, 4)}, device_id_type=MESH
        )

    for slot in range(SLOTS):
        about_ref[slot, 0:1, :] = taps_ref[slot : slot + 1, :ROOT]
        about_ref[slot, 1:2, :] = taps_ref[slot : slot + 1, ROOT:]
        about_ref[slot, 2:3, :] = jnp.full((1, ROOT), water_ref[slot] * float(COARSE * ROOT), jnp.float32)
        about_ref[slot, 3:4, :] = jnp.full((1, ROOT), (live_ref[0] > slot).astype(jnp.float32), jnp.float32)
        for s in range(SEG):
            first = start_ref[slot, s]
            after = first + length_ref[slot, s]
            about_ref[slot, 4 + s : 5 + s, :] = jnp.full((1, ROOT), first.astype(jnp.float32), jnp.float32)
            about_ref[slot, 8 + s : 9 + s, :] = jnp.full((1, ROOT), after.astype(jnp.float32), jnp.float32)
        about_ref[slot, 12:16, :] = jnp.zeros((4, ROOT), jnp.float32)

    pl.semaphore_wait(barrier, 4 + 2 * upper_chip)

    def copies(order, slot, buffer, steps, target):
        where = {"sta": block(steps), "freq": target}
        return [
            pltpu.make_async_remote_copy(
                src_ref=src.at[slot],
                dst_ref=dst.at[buffer],
                send_sem=send_sem.at[order, which],
                recv_sem=recv_sem.at[buffer, which],
                device_id=where,
                device_id_type=MESH,
            )
            for which, (src, dst) in enumerate(((about_ref, far_about_ref), (wave_ref, far_wave_ref)))
        ]

    def for_upper():
        return (
            copies(0, core, 0, 1, core)
            + copies(1, 2 + core, 0, 1, 2 + core)
            + copies(2, core, 1, 2, core)
        )

    def for_lower():
        return copies(0, 2 + core, 1, 2, 2 + core)

    @pl.when(upper_chip == 1)
    def _():
        for copy in for_upper():
            copy.start()

    @pl.when(upper_chip == 0)
    def _():
        for copy in for_lower():
            copy.start()

    first_table = first_ref[...]
    outer_table = outer_ref[...]

    def own_step(slot, carry):
        found = spectra(wave_ref[slot], about_ref[slot], first_ref[...], twiddle_ref, square_ref)
        for s in range(SEG):
            own_ref[slot, s, 0], own_ref[slot, s, 1] = found[s]
        return carry

    lax.fori_loop(0, SLOTS, own_step, 0)

    def exchange(round_index, step):
        target = lax.rem(freq + step, 4)
        return pltpu.make_async_remote_copy(
            src_ref=part_ref.at[round_index, target],
            dst_ref=got_ref.at[round_index, freq],
            send_sem=part_send_sem.at[round_index, step],
            recv_sem=part_recv_sem.at[round_index, step],
            device_id={"sta": sta, "freq": target},
            device_id_type=MESH,
        )

    for r in range(ROUNDS):
        for copy in copies(0, 0, r, 0, 0):
            copy.wait_recv()
        far = spectra(far_wave_ref[r], far_about_ref[r], first_table, twiddle_ref, square_ref)
        pairs = []
        for i in range(SLOTS):
            cross_re = 0.0
            cross_im = 0.0
            for s in range(SEG):
                own_re, own_im = own_ref[i, s, 0], own_ref[i, s, 1]
                far_re, far_im = far[s]
                cross_re = cross_re + own_re * far_re + own_im * far_im
                cross_im = cross_im + own_im * far_re - own_re * far_im
            pairs.append(jnp.concatenate([cross_re, cross_im], axis=1))
        inner = dot(jnp.concatenate(pairs, axis=0).astype(jnp.bfloat16), square_ref[2])
        columns = []
        for i in range(SLOTS):
            inner_re = inner[i * KEPT : (i + 1) * KEPT, :ROOT]
            inner_im = inner[i * KEPT : (i + 1) * KEPT, ROOT:]
            cos_t, sin_t = twiddle_ref[2], twiddle_ref[3]
            columns.append(
                jnp.concatenate(
                    [inner_re * cos_t - inner_im * sin_t, inner_re * sin_t + inner_im * cos_t], axis=0
                ).astype(jnp.bfloat16)
            )
        lagged = dot(outer_table, jnp.concatenate(columns, axis=1))
        for g in range(4):
            band = lagged[g * BAND : (g + 1) * BAND]
            part_ref[r, g] = jnp.concatenate(
                [band[:, i * ROOT : (i + 1) * ROOT] for i in range(SLOTS)], axis=0
            ).astype(jnp.bfloat16)
        for step in (2, 1, 3):
            exchange(r, step).start()
        got_ref[r, freq] = part_ref[r, freq]

    for r in range(ROUNDS):
        for step in (1, 2, 3):
            exchange(r, step).wait_recv()
        for j in range(SLOTS):
            piece = got_ref[r, j].astype(jnp.float32)
            for i in range(SLOTS):
                rows_ref[r, pl.ds(SLOTS * i + j, BAND, stride=SLOTS * SLOTS), :] = piece[i * BAND : (i + 1) * BAND]
        out_ref[r] = rows_ref[r].astype(jnp.bfloat16)

    for r in range(ROUNDS):
        for step in (1, 2, 3):
            exchange(r, step).wait_send()

    @pl.when(upper_chip == 1)
    def _():
        for copy in for_upper():
            copy.wait_send()

    @pl.when(upper_chip == 0)
    def _():
        for copy in for_lower():
            copy.wait_send()


def on_device(waveforms, fir_taps, water_level, gap_start, gap_length, live_slots):
    n_sta = lax.axis_size("sta")
    tables = [jnp.asarray(table) for table in make_tables()]
    wave = waveforms.reshape(SLOTS, SEG, COARSE, ROOT)
    vmem = pl.BlockSpec(memory_space=pltpu.VMEM)
    smem = pl.BlockSpec(memory_space=pltpu.SMEM)
    rows = BAND * SLOTS * SLOTS
    result = pl.pallas_call(
        functools.partial(kernel, n_sta),
        out_shape=jax.ShapeDtypeStruct((ROUNDS, rows, ROOT), jnp.bfloat16),
        in_specs=[vmem, vmem, smem, smem, smem, smem, vmem, vmem, vmem, vmem],
        out_specs=vmem,
        scratch_shapes=[
            pltpu.VMEM((SLOTS, 16, ROOT), jnp.float32),
            pltpu.VMEM((ROUNDS, SEG, COARSE, ROOT), jnp.bfloat16),
            pltpu.VMEM((ROUNDS, 16, ROOT), jnp.float32),
            pltpu.VMEM((SLOTS, SEG, 2, KEPT, ROOT), jnp.float32),
            pltpu.VMEM((ROUNDS, 4, SLOTS * BAND, ROOT), jnp.bfloat16),
            pltpu.VMEM((ROUNDS, 4, SLOTS * BAND, ROOT), jnp.bfloat16),
            pltpu.VMEM((ROUNDS, rows, ROOT), jnp.float32),
            pltpu.SemaphoreType.DMA((3, 2)),
            pltpu.SemaphoreType.DMA((ROUNDS, 2)),
            pltpu.SemaphoreType.DMA((ROUNDS, 4)),
            pltpu.SemaphoreType.DMA((ROUNDS, 4)),
        ],
        compiler_params=pltpu.CompilerParams(
            collective_id=0, has_side_effects=True, vmem_limit_bytes=40 * 1024 * 1024
        ),
    )(wave, fir_taps, water_level, gap_start, gap_length, live_slots, *tables)
    return result.reshape(ROUNDS, BAND, SLOTS, SLOTS, ROOT)


def solution(mesh):
    in_specs = (
        P("sta", None, None),
        P("sta", None),
        P("sta"),
        P("sta", None),
        P("sta", None),
        P("sta"),
    )
    out_specs = P(None, "freq", "sta", None, None)
    return jax.shard_map(
        on_device, mesh=mesh, in_specs=in_specs, out_specs=out_specs, check_vma=False
    )
```

```python
import functools
import math

import jax
import jax.numpy as jnp
import ml_dtypes
import numpy as np
from jax import lax
from jax.experimental import pallas as pl
from jax.experimental.pallas import tpu as pltpu
from jax.sharding import PartitionSpec as P

ROOT = 128
COARSE = 64
LAGROWS = 96
ROUNDS = 2
SLOTS = 4
SEG = 4
KEPT = 72
BAND = LAGROWS // 4
MESH = pl.DeviceIdType.MESH


def as_bf16(table):
    return table.astype(np.float32).astype(ml_dtypes.bfloat16)


def split_bf16(table):
    upper = as_bf16(table)
    return upper, as_bf16(table - upper.astype(np.float64))


def make_tables():
    kept = np.arange(KEPT)
    live = (kept <= 64).astype(np.float64)[:, None]
    full = np.arange(ROOT)
    angle = 2.0 * math.pi / ROOT
    first = kept[:, None] * np.arange(COARSE)[None, :] * angle
    first = np.concatenate([np.cos(first) * live, -np.sin(first) * live], axis=0)
    first_hi, first_lo = split_bf16(first)
    first_table = np.concatenate([first_hi, first_lo], axis=1)
    twist = kept[:, None] * full[None, :] * (angle / ROOT)
    weight = np.where((kept == 0) | (kept == 64), 1.0, 2.0)[:, None] * live
    weight = weight / math.sqrt(SEG * ROOT * ROOT)
    step = np.broadcast_to(kept[:, None] * angle, (KEPT, ROOT))
    twiddles = np.stack(
        [np.cos(twist), np.sin(twist), np.cos(twist) * weight, np.sin(twist) * weight, np.cos(step), np.sin(step)]
    ).astype(np.float32)
    square = full[:, None] * full[None, :] * angle
    cos_b, sin_b = np.cos(square), np.sin(square)
    last = np.block([[cos_b, -sin_b], [sin_b, cos_b]])
    last_hi, last_lo = split_bf16(last)
    inner = as_bf16(np.block([[cos_b, sin_b], [-sin_b, cos_b]]))
    square_tables = np.stack([last_hi, last_lo, inner])
    lag = (np.arange(LAGROWS) - LAGROWS // 2)[:, None] * kept[None, :] * angle
    outer = as_bf16(np.concatenate([np.cos(lag), -np.sin(lag)], axis=1))
    return first_table, twiddles, square_tables, outer


def dot(left, right):
    return jnp.dot(left, right, preferred_element_type=jnp.float32)


def spectra(wave, about, stage, first_table, twiddles, squares):
    place = (
        lax.broadcasted_iota(jnp.int32, (COARSE, ROOT), 0) * ROOT
        + lax.broadcasted_iota(jnp.int32, (COARSE, ROOT), 1)
    ).astype(jnp.float32)
    wide = wave.astype(jnp.float32)
    for row in range(COARSE):
        stage[SEG * row : SEG * (row + 1), :] = wide[:, row * ROOT : (row + 1) * ROOT]
    records = []
    for s in range(SEG):
        start = about[4 + s : 5 + s, :]
        end = about[8 + s : 9 + s, :]
        gone = (place >= start) & (place < end)
        record = jnp.where(gone, 0.0, stage[pl.ds(s, COARSE, stride=SEG), :])
        records.append(record.astype(jnp.bfloat16))
    record = jnp.concatenate(records, axis=1)
    section = dot(first_table, jnp.concatenate([record, record], axis=0))
    cos_t, sin_t = twiddles[0], twiddles[1]
    tap0 = about[0:1, :]
    tap1 = about[1:2, :]
    rows = [(tap0 + tap1 * twiddles[4], -(tap1 * twiddles[5]))]
    for s in range(SEG):
        columns = section[:, s * ROOT : (s + 1) * ROOT]
        rows.append((columns[:KEPT], columns[KEPT:]))
    twisted = jnp.concatenate(
        [
            jnp.concatenate([re * cos_t + im * sin_t, im * cos_t - re * sin_t], axis=1)
            for re, im in rows
        ],
        axis=0,
    )
    upper = twisted.astype(jnp.bfloat16)
    lower = (twisted - upper.astype(jnp.float32)).astype(jnp.bfloat16)
    bins = dot(upper, squares[0]) + dot(lower, squares[0]) + dot(upper, squares[1])
    resp_re, resp_im = bins[:KEPT, :ROOT], bins[:KEPT, ROOT:]
    water = about[2:3, :]
    alive = about[3:4, :]
    found = []
    for s in range(SEG):
        part = bins[(s + 1) * KEPT : (s + 2) * KEPT]
        spec_re, spec_im = part[:, :ROOT], part[:, ROOT:]
        white_re = resp_re * spec_re - resp_im * spec_im
        white_im = resp_re * spec_im + resp_im * spec_re
        factor = alive * lax.rsqrt(white_re * white_re + white_im * white_im + water)
        found.append((white_re * factor, white_im * factor))
    return found


def kernel(
    n_sta,
    wave_hbm,
    taps_hbm,
    water_hbm,
    start_hbm,
    length_hbm,
    live_hbm,
    first_hbm,
    twiddle_hbm,
    square_hbm,
    outer_hbm,
    out_ref,
    wave_ref,
    taps_ref,
    water_ref,
    start_ref,
    length_ref,
    live_ref,
    first_ref,
    twiddle_ref,
    square_ref,
    outer_ref,
    about_ref,
    far_wave_ref,
    far_about_ref,
    stage_ref,
    own_ref,
    part_ref,
    got_ref,
    rows_ref,
    load_sem,
    send_sem,
    recv_sem,
    part_send_sem,
    part_recv_sem,
):
    sta = lax.axis_index("sta")
    freq = lax.axis_index("freq")
    core = lax.rem(freq, 2)
    upper_chip = freq // 2
    stride = n_sta // (2 * ROUNDS)

    def block(steps):
        return lax.rem(sta + (steps % 4) * stride, n_sta)

    barrier = pltpu.get_barrier_semaphore()
    for steps, source in ((-1, 2), (-1, 3), (-2, 0), (-2, 1)):
        pl.semaphore_signal(
            barrier, inc=1, device_id={"sta": block(steps), "freq": source}, device_id_type=MESH
        )

    small = [
        pltpu.make_async_copy(source, target, load_sem.at[n])
        for n, (source, target) in enumerate(
            (
                (taps_hbm, taps_ref),
                (water_hbm, water_ref),
                (start_hbm, start_ref),
                (length_hbm, length_ref),
                (live_hbm, live_ref),
            )
        )
    ]
    large = [
        pltpu.make_async_copy(source, target, load_sem.at[5 + n])
        for n, (source, target) in enumerate(
            (
                (wave_hbm, wave_ref),
                (first_hbm, first_ref),
                (twiddle_hbm, twiddle_ref),
                (square_hbm, square_ref),
                (outer_hbm, outer_ref),
            )
        )
    ]
    for copy in small + large:
        copy.start()

    pl.semaphore_wait(barrier, 4)

    feeds = {"sta": lax.rem(sta + (2 - upper_chip) * stride, n_sta), "freq": 2 * (1 - upper_chip) + core}

    def send_wave(q):
        return pltpu.make_async_remote_copy(
            src_ref=wave_hbm.at[2 * core + q],
            dst_ref=far_wave_ref.at[q],
            send_sem=send_sem.at[q],
            recv_sem=recv_sem.at[q],
            device_id=feeds,
            device_id_type=MESH,
        )

    def send_about():
        return pltpu.make_async_remote_copy(
            src_ref=about_ref.at[pl.ds(2 * core, 2)],
            dst_ref=far_about_ref,
            send_sem=send_sem.at[2],
            recv_sem=recv_sem.at[2],
            device_id=feeds,
            device_id_type=MESH,
        )

    waits = (1 - upper_chip) * lax.rem(sta // stride, 2)

    @pl.when(waits == 0)
    def _():
        send_wave(0).start()

    for copy in small:
        copy.wait()

    for slot in range(SLOTS):
        about_ref[slot, 0:1, :] = taps_ref[slot : slot + 1, :ROOT]
        about_ref[slot, 1:2, :] = taps_ref[slot : slot + 1, ROOT:]
        about_ref[slot, 2:3, :] = jnp.full((1, ROOT), water_ref[slot] * float(COARSE * ROOT), jnp.float32)
        about_ref[slot, 3:4, :] = jnp.full((1, ROOT), (live_ref[0] > slot).astype(jnp.float32), jnp.float32)
        for s in range(SEG):
            first = start_ref[slot, s]
            after = first + length_ref[slot, s]
            about_ref[slot, 4 + s : 5 + s, :] = jnp.full((1, ROOT), first.astype(jnp.float32), jnp.float32)
            about_ref[slot, 8 + s : 9 + s, :] = jnp.full((1, ROOT), after.astype(jnp.float32), jnp.float32)
        about_ref[slot, 12:16, :] = jnp.zeros((4, ROOT), jnp.float32)

    @pl.when(waits == 0)
    def _():
        send_about().start()
        send_wave(1).start()

    for copy in large:
        copy.wait()

    first_table = first_ref[...]
    outer_table = outer_ref[...]

    def own_step(slot, carry):
        found = spectra(
            wave_ref[slot], about_ref[slot], stage_ref, first_ref[...], twiddle_ref, square_ref
        )
        for s in range(SEG):
            own_ref[slot, s, 0], own_ref[slot, s, 1] = found[s]
        return carry

    lax.fori_loop(0, SLOTS, own_step, 0)

    @pl.when(waits == 1)
    def _():
        send_wave(0).start()
        send_about().start()
        send_wave(1).start()

    def exchange(q, step):
        target = lax.rem(freq + step, 4)
        return pltpu.make_async_remote_copy(
            src_ref=part_ref.at[q, target],
            dst_ref=got_ref.at[upper_chip, 2 * core + q],
            send_sem=part_send_sem.at[q, step],
            recv_sem=part_recv_sem.at[q, step],
            device_id={"sta": sta, "freq": target},
            device_id_type=MESH,
        )

    for q in range(2):
        if q == 0:
            pltpu.make_async_copy(far_about_ref, far_about_ref, recv_sem.at[2]).wait()
        pltpu.make_async_copy(far_wave_ref.at[q], far_wave_ref.at[q], recv_sem.at[q]).wait()
        far = spectra(
            far_wave_ref[q], far_about_ref[q], stage_ref, first_table, twiddle_ref, square_ref
        )
        pairs = []
        for i in range(SLOTS):
            cross_re = 0.0
            cross_im = 0.0
            for s in range(SEG):
                own_re, own_im = own_ref[i, s, 0], own_ref[i, s, 1]
                far_re, far_im = far[s]
                cross_re = cross_re + own_re * far_re + own_im * far_im
                cross_im = cross_im + own_im * far_re - own_re * far_im
            pairs.append(jnp.concatenate([cross_re, cross_im], axis=1))
        inner = dot(jnp.concatenate(pairs, axis=0).astype(jnp.bfloat16), square_ref[2])
        columns = []
        for i in range(SLOTS):
            inner_re = inner[i * KEPT : (i + 1) * KEPT, :ROOT]
            inner_im = inner[i * KEPT : (i + 1) * KEPT, ROOT:]
            cos_t, sin_t = twiddle_ref[2], twiddle_ref[3]
            columns.append(
                jnp.concatenate(
                    [inner_re * cos_t - inner_im * sin_t, inner_re * sin_t + inner_im * cos_t], axis=0
                ).astype(jnp.bfloat16)
            )
        lagged = dot(outer_table, jnp.concatenate(columns, axis=1))
        for g in range(4):
            band = lagged[g * BAND : (g + 1) * BAND]
            part_ref[q, g] = jnp.concatenate(
                [band[:, i * ROOT : (i + 1) * ROOT] for i in range(SLOTS)], axis=0
            ).astype(jnp.bfloat16)
        for step in (2, 1, 3):
            exchange(q, step).start()
        got_ref[upper_chip, 2 * core + q] = part_ref[q, freq]

    for q in range(2):
        for step in (1, 2, 3):
            exchange(q, step).wait_recv()
    for r in range(ROUNDS):
        for j in range(SLOTS):
            piece = got_ref[r, j].astype(jnp.float32)
            for i in range(SLOTS):
                rows_ref[r, pl.ds(SLOTS * i + j, BAND, stride=SLOTS * SLOTS), :] = piece[i * BAND : (i + 1) * BAND]
        out_ref[r] = rows_ref[r].astype(jnp.bfloat16)

    for q in range(2):
        for step in (1, 2, 3):
            exchange(q, step).wait_send()
        send_wave(q).wait_send()
    send_about().wait_send()


def on_device(waveforms, fir_taps, water_level, gap_start, gap_length, live_slots):
    n_sta = lax.axis_size("sta")
    tables = [jnp.asarray(table) for table in make_tables()]
    anywhere = pl.BlockSpec(memory_space=pl.ANY)
    rows = BAND * SLOTS * SLOTS
    result = pl.pallas_call(
        functools.partial(kernel, n_sta),
        out_shape=jax.ShapeDtypeStruct((ROUNDS, rows, ROOT), jnp.bfloat16),
        in_specs=[anywhere] * 10,
        out_specs=pl.BlockSpec(memory_space=pltpu.VMEM),
        scratch_shapes=[
            pltpu.VMEM((SLOTS, SEG, COARSE * ROOT), jnp.bfloat16),
            pltpu.VMEM((SLOTS, 2 * ROOT), jnp.float32),
            pltpu.SMEM((SLOTS,), jnp.float32),
            pltpu.SMEM((SLOTS, SEG), jnp.int32),
            pltpu.SMEM((SLOTS, SEG), jnp.int32),
            pltpu.SMEM((1,), jnp.int32),
        ]
        + [pltpu.VMEM(table.shape, table.dtype) for table in tables]
        + [
            pltpu.VMEM((SLOTS, 16, ROOT), jnp.float32),
            pltpu.VMEM((2, SEG, COARSE * ROOT), jnp.bfloat16),
            pltpu.VMEM((2, 16, ROOT), jnp.float32),
            pltpu.VMEM((SEG * COARSE, ROOT), jnp.float32),
            pltpu.VMEM((SLOTS, SEG, 2, KEPT, ROOT), jnp.float32),
            pltpu.VMEM((2, 4, SLOTS * BAND, ROOT), jnp.bfloat16),
            pltpu.VMEM((ROUNDS, SLOTS, SLOTS * BAND, ROOT), jnp.bfloat16),
            pltpu.VMEM((ROUNDS, rows, ROOT), jnp.float32),
            pltpu.SemaphoreType.DMA((10,)),
            pltpu.SemaphoreType.DMA((3,)),
            pltpu.SemaphoreType.DMA((3,)),
            pltpu.SemaphoreType.DMA((2, 4)),
            pltpu.SemaphoreType.DMA((2, 4)),
        ],
        compiler_params=pltpu.CompilerParams(
            collective_id=0, has_side_effects=True, vmem_limit_bytes=56 * 1024 * 1024
        ),
    )(waveforms, fir_taps, water_level, gap_start, gap_length, live_slots, *tables)
    return result.reshape(ROUNDS, BAND, SLOTS, SLOTS, ROOT)


def solution(mesh):
    in_specs = (
        P("sta", None, None),
        P("sta", None),
        P("sta"),
        P("sta", None),
        P("sta", None),
        P("sta"),
    )
    out_specs = P(None, "freq", "sta", None, None)
    return jax.shard_map(
        on_device, mesh=mesh, in_specs=in_specs, out_specs=out_specs, check_vma=False
    )
```

```python
import functools
import math

import jax
import jax.numpy as jnp
import ml_dtypes
import numpy as np
from jax import lax
from jax.experimental import pallas as pl
from jax.experimental.pallas import tpu as pltpu
from jax.sharding import PartitionSpec as P

ROOT = 128
COARSE = 64
LAGROWS = 96
ROUNDS = 2
SLOTS = 4
SEG = 4
KEPT = 72
BAND = LAGROWS // 4
MESH = pl.DeviceIdType.MESH


def as_bf16(table):
    return table.astype(np.float32).astype(ml_dtypes.bfloat16)


def split_bf16(table):
    upper = as_bf16(table)
    return upper, as_bf16(table - upper.astype(np.float64))


def make_tables():
    kept = np.arange(KEPT)
    live = (kept <= 64).astype(np.float64)[:, None]
    full = np.arange(ROOT)
    angle = 2.0 * math.pi / ROOT
    first = kept[:, None] * np.arange(COARSE)[None, :] * angle
    first = np.concatenate([np.cos(first) * live, -np.sin(first) * live], axis=0)
    first_hi, first_lo = split_bf16(first)
    first_table = np.concatenate([first_hi, first_lo], axis=1)
    twist = kept[:, None] * full[None, :] * (angle / ROOT)
    weight = np.where((kept == 0) | (kept == 64), 1.0, 2.0)[:, None] * live
    weight = weight / math.sqrt(SEG * ROOT * ROOT)
    step = np.broadcast_to(kept[:, None] * angle, (KEPT, ROOT))
    twiddles = np.stack(
        [np.cos(twist), np.sin(twist), np.cos(twist) * weight, np.sin(twist) * weight, np.cos(step), np.sin(step)]
    ).astype(np.float32)
    square = full[:, None] * full[None, :] * angle
    cos_b, sin_b = np.cos(square), np.sin(square)
    last = np.block([[cos_b, -sin_b], [sin_b, cos_b]])
    last_hi, last_lo = split_bf16(last)
    inner = as_bf16(np.block([[cos_b, sin_b], [-sin_b, cos_b]]))
    square_tables = np.stack([last_hi, last_lo, inner])
    lag = (np.arange(LAGROWS) - LAGROWS // 2)[:, None] * kept[None, :] * angle
    outer = as_bf16(np.concatenate([np.cos(lag), -np.sin(lag)], axis=1))
    return first_table, twiddles, square_tables, outer


def dot(left, right):
    return jnp.dot(left, right, preferred_element_type=jnp.float32)


def spectra(wave, about, stage, first_table, twiddles, squares):
    place = (
        lax.broadcasted_iota(jnp.int32, (COARSE, ROOT), 0) * ROOT
        + lax.broadcasted_iota(jnp.int32, (COARSE, ROOT), 1)
    ).astype(jnp.float32)
    wide = wave.astype(jnp.float32)
    for row in range(COARSE):
        stage[SEG * row : SEG * (row + 1), :] = wide[:, row * ROOT : (row + 1) * ROOT]
    records = []
    for s in range(SEG):
        start = about[4 + s : 5 + s, :]
        end = about[8 + s : 9 + s, :]
        gone = (place >= start) & (place < end)
        record = jnp.where(gone, 0.0, stage[pl.ds(s, COARSE, stride=SEG), :])
        records.append(record.astype(jnp.bfloat16))
    record = jnp.concatenate(records, axis=1)
    section = dot(first_table, jnp.concatenate([record, record], axis=0))
    cos_t, sin_t = twiddles[0], twiddles[1]
    tap0 = about[0:1, :]
    tap1 = about[1:2, :]
    rows = [(tap0 + tap1 * twiddles[4], -(tap1 * twiddles[5]))]
    for s in range(SEG):
        columns = section[:, s * ROOT : (s + 1) * ROOT]
        rows.append((columns[:KEPT], columns[KEPT:]))
    twisted = jnp.concatenate(
        [
            jnp.concatenate([re * cos_t + im * sin_t, im * cos_t - re * sin_t], axis=1)
            for re, im in rows
        ],
        axis=0,
    )
    upper = twisted.astype(jnp.bfloat16)
    lower = (twisted - upper.astype(jnp.float32)).astype(jnp.bfloat16)
    bins = dot(upper, squares[0]) + dot(lower, squares[0]) + dot(upper, squares[1])
    resp_re, resp_im = bins[:KEPT, :ROOT], bins[:KEPT, ROOT:]
    water = about[2:3, :]
    alive = about[3:4, :]
    found = []
    for s in range(SEG):
        part = bins[(s + 1) * KEPT : (s + 2) * KEPT]
        spec_re, spec_im = part[:, :ROOT], part[:, ROOT:]
        white_re = resp_re * spec_re - resp_im * spec_im
        white_im = resp_re * spec_im + resp_im * spec_re
        factor = alive * lax.rsqrt(white_re * white_re + white_im * white_im + water)
        found.append((white_re * factor, white_im * factor))
    return found


def kernel(
    n_sta,
    wave_hbm,
    taps_hbm,
    water_hbm,
    start_hbm,
    length_hbm,
    live_hbm,
    first_hbm,
    twiddle_hbm,
    square_hbm,
    outer_hbm,
    out_ref,
    wave_ref,
    taps_ref,
    water_ref,
    start_ref,
    length_ref,
    live_ref,
    first_ref,
    twiddle_ref,
    square_ref,
    outer_ref,
    about_ref,
    far_wave_ref,
    far_about_ref,
    stage_ref,
    own_ref,
    part_ref,
    got_ref,
    rows_ref,
    load_sem,
    send_sem,
    recv_sem,
    part_send_sem,
    part_recv_sem,
):
    sta = lax.axis_index("sta")
    freq = lax.axis_index("freq")
    core = lax.rem(freq, 2)
    chip = freq // 2
    stride = n_sta // (2 * ROUNDS)
    odd = lax.rem(sta // stride, 2)

    def device(steps, index):
        return {"sta": lax.rem(sta + (steps % 4) * stride, n_sta), "freq": index}

    barrier = pltpu.get_barrier_semaphore()

    def signal(where):
        pl.semaphore_signal(barrier, inc=1, device_id=where, device_id_type=MESH)

    signal(device(-1, 3))
    signal(device(-2, jnp.where(chip == 0, 2 + odd, 0)))

    @pl.when(chip == 1)
    def _():
        signal(device(-2, 1))

    small = [
        pltpu.make_async_copy(source, target, load_sem.at[n])
        for n, (source, target) in enumerate(
            (
                (taps_hbm, taps_ref),
                (water_hbm, water_ref),
                (start_hbm, start_ref),
                (length_hbm, length_ref),
                (live_hbm, live_ref),
            )
        )
    ]
    large = [
        pltpu.make_async_copy(source, target, load_sem.at[5 + n])
        for n, (source, target) in enumerate(
            (
                (wave_hbm, wave_ref),
                (first_hbm, first_ref),
                (twiddle_hbm, twiddle_ref),
                (square_hbm, square_ref),
                (outer_hbm, outer_ref),
            )
        )
    ]
    feeds_next = (chip == 1) & (core == 1)
    group = sta // stride
    feeds_second = (chip == 1) & (core == 0) & (odd == 0) & (group != 0)
    feeds_second_late = (chip == 1) & (core == 0) & (group == 0)
    feeds_back = (chip == 0) & (odd == 0)
    feeds_late = (chip == 0) & (odd == 1)
    relays = feeds_back
    expected = jnp.where(chip == 0, 2, jnp.where(core == 1, 4 + 2 * odd, 2))

    @pl.when((chip == 0) | (core == 1) | (odd == 0))
    def _():
        pl.semaphore_wait(barrier, expected)

    def wave_to(where, slot, place, order):
        return pltpu.make_async_remote_copy(
            src_ref=wave_hbm.at[slot],
            dst_ref=far_wave_ref.at[place],
            send_sem=send_sem.at[order],
            recv_sem=recv_sem.at[place],
            device_id=where,
            device_id_type=MESH,
        )

    def about_to(where, slot, round_index, order):
        return pltpu.make_async_remote_copy(
            src_ref=about_ref.at[pl.ds(slot, 2)],
            dst_ref=far_about_ref.at[round_index],
            send_sem=send_sem.at[order],
            recv_sem=recv_sem.at[4 + round_index],
            device_id=where,
            device_id_type=MESH,
        )

    def sends(steps, round_index):
        targets = [device(steps, c) for c in range(2)]
        return (
            [wave_to(targets[c], 2 * c, 2 * round_index, c) for c in range(2)],
            [about_to(targets[c], 2 * c, round_index, 4 + c) for c in range(2)]
            + [wave_to(targets[c], 2 * c + 1, 2 * round_index + 1, 2 + c) for c in range(2)],
        )

    def sends_back():
        target = device(2, 2 + core)
        return (
            [wave_to(target, 2 * core, 2, 0)],
            [about_to(target, 2 * core, 1, 4), wave_to(target, 2 * core + 1, 3, 1)],
        )

    def start(copies):
        for copy in copies:
            copy.start()

    @pl.when(feeds_next)
    def _():
        start(sends(1, 0)[0])

    @pl.when(feeds_second)
    def _():
        start(sends(2, 1)[0])

    @pl.when(feeds_back)
    def _():
        start(sends_back()[0])

    for copy in small + large:
        copy.start()
    for copy in small:
        copy.wait()

    for slot in range(SLOTS):
        about_ref[slot, 0:1, :] = taps_ref[slot : slot + 1, :ROOT]
        about_ref[slot, 1:2, :] = taps_ref[slot : slot + 1, ROOT:]
        about_ref[slot, 2:3, :] = jnp.full((1, ROOT), water_ref[slot] * float(COARSE * ROOT), jnp.float32)
        about_ref[slot, 3:4, :] = jnp.full((1, ROOT), (live_ref[0] > slot).astype(jnp.float32), jnp.float32)
        for s in range(SEG):
            first = start_ref[slot, s]
            after = first + length_ref[slot, s]
            about_ref[slot, 4 + s : 5 + s, :] = jnp.full((1, ROOT), first.astype(jnp.float32), jnp.float32)
            about_ref[slot, 8 + s : 9 + s, :] = jnp.full((1, ROOT), after.astype(jnp.float32), jnp.float32)
        about_ref[slot, 12:16, :] = jnp.zeros((4, ROOT), jnp.float32)

    @pl.when(feeds_next)
    def _():
        start(sends(1, 0)[1])

    @pl.when(feeds_second)
    def _():
        start(sends(2, 1)[1])

    @pl.when(feeds_back)
    def _():
        start(sends_back()[1])

    for copy in large:
        copy.wait()

    turn = jnp.where(group == 1, SLOTS - 1, 1)

    def own_step(slot, carry):
        @pl.when(feeds_late & (slot == turn))
        def _():
            start(sends_back()[0] + sends_back()[1])

        @pl.when(feeds_second_late & (slot == 1))
        def _():
            start(sends(2, 1)[0] + sends(2, 1)[1])

        found = spectra(
            wave_ref[slot], about_ref[slot], stage_ref, first_ref[...], twiddle_ref, square_ref
        )
        for s in range(SEG):
            own_ref[slot, s, 0], own_ref[slot, s, 1] = found[s]
        return carry

    lax.fori_loop(0, SLOTS, own_step, 0)

    def relay(q):
        copies = [
            pltpu.make_async_remote_copy(
                src_ref=far_wave_ref.at[q],
                dst_ref=far_wave_ref.at[2 + q],
                send_sem=send_sem.at[6 + q],
                recv_sem=recv_sem.at[2 + q],
                device_id=device(1, core),
                device_id_type=MESH,
            )
        ]
        if q == 0:
            copies.append(
                pltpu.make_async_remote_copy(
                    src_ref=far_about_ref.at[0],
                    dst_ref=far_about_ref.at[1],
                    send_sem=send_sem.at[8],
                    recv_sem=recv_sem.at[5],
                    device_id=device(1, core),
                    device_id_type=MESH,
                )
            )
        return copies

    def share(place, target):
        return pltpu.make_async_remote_copy(
            src_ref=part_ref.at[place, target],
            dst_ref=got_ref.at[place // 2, 2 * core + lax.rem(place, 2)],
            send_sem=part_send_sem.at[place, target],
            recv_sem=part_recv_sem.at[place // 2, 2 * core + lax.rem(place, 2)],
            device_id=device(0, target),
            device_id_type=MESH,
        )

    def far_step(place, carry):
        round_index = place // 2
        q = lax.rem(place, 2)

        @pl.when(q == 0)
        def _():
            pltpu.make_async_copy(
                far_about_ref.at[round_index], far_about_ref.at[round_index], recv_sem.at[4 + round_index]
            ).wait()

        pltpu.make_async_copy(far_wave_ref.at[place], far_wave_ref.at[place], recv_sem.at[place]).wait()
        for early in range(2):

            @pl.when(relays & (place == early))
            def _(early=early):
                start(relay(early))

        far = spectra(
            far_wave_ref[place],
            far_about_ref.at[round_index, q],
            stage_ref,
            first_ref[...],
            twiddle_ref,
            square_ref,
        )
        pairs = []
        for i in range(SLOTS):
            cross_re = 0.0
            cross_im = 0.0
            for s in range(SEG):
                own_re, own_im = own_ref[i, s, 0], own_ref[i, s, 1]
                far_re, far_im = far[s]
                cross_re = cross_re + own_re * far_re + own_im * far_im
                cross_im = cross_im + own_im * far_re - own_re * far_im
            pairs.append(jnp.concatenate([cross_re, cross_im], axis=1))
        inner = dot(jnp.concatenate(pairs, axis=0).astype(jnp.bfloat16), square_ref[2])
        columns = []
        for i in range(SLOTS):
            inner_re = inner[i * KEPT : (i + 1) * KEPT, :ROOT]
            inner_im = inner[i * KEPT : (i + 1) * KEPT, ROOT:]
            cos_t, sin_t = twiddle_ref[2], twiddle_ref[3]
            columns.append(
                jnp.concatenate(
                    [inner_re * cos_t - inner_im * sin_t, inner_re * sin_t + inner_im * cos_t], axis=0
                ).astype(jnp.bfloat16)
            )
        lagged = dot(outer_ref[...], jnp.concatenate(columns, axis=1))
        for g in range(4):
            band = lagged[g * BAND : (g + 1) * BAND]
            part_ref[place, g] = jnp.concatenate(
                [band[:, i * ROOT : (i + 1) * ROOT] for i in range(SLOTS)], axis=0
            ).astype(jnp.bfloat16)

        @pl.when(place < 2)
        def _():
            for target in (2, 3):
                share(place, target).start()

        share(place, freq + 1 - 2 * core).start()
        got_ref[round_index, 2 * core + q] = part_ref[place, freq]
        return carry

    lax.fori_loop(2 * chip, 4, far_step, 0)

    def arrived(round_index, slot):
        pltpu.make_async_copy(
            got_ref.at[round_index, slot], got_ref.at[round_index, slot], part_recv_sem.at[round_index, slot]
        ).wait()

    for r in range(ROUNDS):
        for q in range(2):
            arrived(r, 2 * (1 - core) + q)
        if r == 0:

            @pl.when(chip == 1)
            def _():
                for q in range(2):
                    arrived(0, 2 * core + q)

        for j in range(SLOTS):
            piece = got_ref[r, j].astype(jnp.float32)
            for i in range(SLOTS):
                rows_ref[r, pl.ds(SLOTS * i + j, BAND, stride=SLOTS * SLOTS), :] = piece[i * BAND : (i + 1) * BAND]
        out_ref[r] = rows_ref[r].astype(jnp.bfloat16)

    def finish(copies):
        for copy in copies:
            copy.wait_send()

    def sent(place, carry):
        @pl.when(place < 2)
        def _():
            for target in (2, 3):
                share(place, target).wait_send()

        share(place, freq + 1 - 2 * core).wait_send()
        return carry

    lax.fori_loop(2 * chip, 4, sent, 0)

    @pl.when(feeds_next)
    def _():
        finish(sends(1, 0)[0] + sends(1, 0)[1])

    @pl.when(feeds_second | feeds_second_late)
    def _():
        finish(sends(2, 1)[0] + sends(2, 1)[1])

    @pl.when(chip == 0)
    def _():
        finish(sends_back()[0] + sends_back()[1])

    @pl.when(relays)
    def _():
        finish(relay(0) + relay(1))


def on_device(waveforms, fir_taps, water_level, gap_start, gap_length, live_slots):
    n_sta = lax.axis_size("sta")
    tables = [jnp.asarray(table) for table in make_tables()]

    def pinned(*arrays):
        return [pltpu.with_memory_space_constraint(array, pltpu.HBM) for array in arrays]

    anywhere = pl.BlockSpec(memory_space=pl.ANY)
    rows = BAND * SLOTS * SLOTS
    result = pl.pallas_call(
        functools.partial(kernel, n_sta),
        out_shape=jax.ShapeDtypeStruct((ROUNDS, rows, ROOT), jnp.bfloat16),
        in_specs=[anywhere] * 10,
        out_specs=pl.BlockSpec(memory_space=pltpu.VMEM),
        scratch_shapes=[
            pltpu.VMEM((SLOTS, SEG, COARSE * ROOT), jnp.bfloat16),
            pltpu.VMEM((SLOTS, 2 * ROOT), jnp.float32),
            pltpu.SMEM((SLOTS,), jnp.float32),
            pltpu.SMEM((SLOTS, SEG), jnp.int32),
            pltpu.SMEM((SLOTS, SEG), jnp.int32),
            pltpu.SMEM((1,), jnp.int32),
        ]
        + [pltpu.VMEM(table.shape, table.dtype) for table in tables]
        + [
            pltpu.VMEM((SLOTS, 16, ROOT), jnp.float32),
            pltpu.VMEM((4, SEG, COARSE * ROOT), jnp.bfloat16),
            pltpu.VMEM((ROUNDS, 2, 16, ROOT), jnp.float32),
            pltpu.VMEM((SEG * COARSE, ROOT), jnp.float32),
            pltpu.VMEM((SLOTS, SEG, 2, KEPT, ROOT), jnp.float32),
            pltpu.VMEM((4, 4, SLOTS * BAND, ROOT), jnp.bfloat16),
            pltpu.VMEM((ROUNDS, SLOTS, SLOTS * BAND, ROOT), jnp.bfloat16),
            pltpu.VMEM((ROUNDS, rows, ROOT), jnp.float32),
            pltpu.SemaphoreType.DMA((10,)),
            pltpu.SemaphoreType.DMA((9,)),
            pltpu.SemaphoreType.DMA((6,)),
            pltpu.SemaphoreType.DMA((4, 4)),
            pltpu.SemaphoreType.DMA((ROUNDS, SLOTS)),
        ],
        compiler_params=pltpu.CompilerParams(
            collective_id=0, has_side_effects=True, vmem_limit_bytes=40 * 1024 * 1024
        ),
    )(
        *pinned(waveforms, fir_taps, water_level, gap_start, gap_length), live_slots, *pinned(*tables)
    )
    return result.reshape(ROUNDS, BAND, SLOTS, SLOTS, ROOT)


def solution(mesh):
    in_specs = (
        P("sta", None, None),
        P("sta", None),
        P("sta"),
        P("sta", None),
        P("sta", None),
        P("sta"),
    )
    out_specs = P(None, "freq", "sta", None, None)
    return jax.shard_map(
        on_device, mesh=mesh, in_specs=in_specs, out_specs=out_specs, check_vma=False
    )
```

```python
import functools
import math

import jax
import jax.numpy as jnp
import ml_dtypes
import numpy as np
from jax import lax
from jax.experimental import pallas as pl
from jax.experimental.pallas import tpu as pltpu
from jax.sharding import PartitionSpec as P

ROOT = 128
COARSE = 64
LAGROWS = 96
ROUNDS = 2
SLOTS = 4
SEG = 4
KEPT = 72
BAND = LAGROWS // 4
MESH = pl.DeviceIdType.MESH


def as_bf16(table):
    return table.astype(np.float32).astype(ml_dtypes.bfloat16)


def split_bf16(table):
    upper = as_bf16(table)
    return upper, as_bf16(table - upper.astype(np.float64))


def make_tables():
    kept = np.arange(KEPT)
    live = (kept <= 64).astype(np.float64)[:, None]
    full = np.arange(ROOT)
    angle = 2.0 * math.pi / ROOT
    first = kept[:, None] * np.arange(COARSE)[None, :] * angle
    first = np.concatenate([np.cos(first) * live, -np.sin(first) * live], axis=0)
    first_hi, first_lo = split_bf16(first)
    first_table = np.concatenate([first_hi, first_lo], axis=1)
    twist = kept[:, None] * full[None, :] * (angle / ROOT)
    weight = np.where((kept == 0) | (kept == 64), 1.0, 2.0)[:, None] * live
    weight = weight / math.sqrt(SEG * ROOT * ROOT)
    step = np.broadcast_to(kept[:, None] * angle, (KEPT, ROOT))
    twiddles = np.stack(
        [np.cos(twist), np.sin(twist), np.cos(twist) * weight, np.sin(twist) * weight, np.cos(step), np.sin(step)]
    ).astype(np.float32)
    square = full[:, None] * full[None, :] * angle
    cos_b, sin_b = np.cos(square), np.sin(square)
    last = np.block([[cos_b, -sin_b], [sin_b, cos_b]])
    last_hi, last_lo = split_bf16(last)
    inner = as_bf16(np.block([[cos_b, sin_b], [-sin_b, cos_b]]))
    square_tables = np.stack([last_hi, last_lo, inner])
    lag = (np.arange(LAGROWS) - LAGROWS // 2)[:, None] * kept[None, :] * angle
    outer = as_bf16(np.concatenate([np.cos(lag), -np.sin(lag)], axis=1))
    return first_table, twiddles, square_tables, outer


def dot(left, right):
    return jnp.dot(left, right, preferred_element_type=jnp.float32)


def spectra(wave, about, stage, first_table, twiddles, squares):
    place = (
        lax.broadcasted_iota(jnp.int32, (COARSE, ROOT), 0) * ROOT
        + lax.broadcasted_iota(jnp.int32, (COARSE, ROOT), 1)
    ).astype(jnp.float32)
    wide = wave.astype(jnp.float32)
    for row in range(COARSE):
        stage[SEG * row : SEG * (row + 1), :] = wide[:, row * ROOT : (row + 1) * ROOT]
    records = []
    for s in range(SEG):
        start = about[4 + s : 5 + s, :]
        end = about[8 + s : 9 + s, :]
        gone = (place >= start) & (place < end)
        record = jnp.where(gone, 0.0, stage[pl.ds(s, COARSE, stride=SEG), :])
        records.append(record.astype(jnp.bfloat16))
    record = jnp.concatenate(records, axis=1)
    section = dot(first_table, jnp.concatenate([record, record], axis=0))
    cos_t, sin_t = twiddles[0], twiddles[1]
    tap0 = about[0:1, :]
    tap1 = about[1:2, :]
    rows = [(tap0 + tap1 * twiddles[4], -(tap1 * twiddles[5]))]
    for s in range(SEG):
        columns = section[:, s * ROOT : (s + 1) * ROOT]
        rows.append((columns[:KEPT], columns[KEPT:]))
    twisted = jnp.concatenate(
        [
            jnp.concatenate([re * cos_t + im * sin_t, im * cos_t - re * sin_t], axis=1)
            for re, im in rows
        ],
        axis=0,
    )
    upper = twisted.astype(jnp.bfloat16)
    lower = (twisted - upper.astype(jnp.float32)).astype(jnp.bfloat16)
    bins = dot(upper, squares[0]) + dot(lower, squares[0]) + dot(upper, squares[1])
    resp_re, resp_im = bins[:KEPT, :ROOT], bins[:KEPT, ROOT:]
    water = about[2:3, :]
    alive = about[3:4, :]
    found = []
    for s in range(SEG):
        part = bins[(s + 1) * KEPT : (s + 2) * KEPT]
        spec_re, spec_im = part[:, :ROOT], part[:, ROOT:]
        white_re = resp_re * spec_re - resp_im * spec_im
        white_im = resp_re * spec_im + resp_im * spec_re
        factor = alive * lax.rsqrt(white_re * white_re + white_im * white_im + water)
        found.append((white_re * factor, white_im * factor))
    return found


def kernel(
    n_sta,
    wave_hbm,
    taps_hbm,
    water_hbm,
    start_hbm,
    length_hbm,
    live_hbm,
    first_hbm,
    twiddle_hbm,
    square_hbm,
    outer_hbm,
    out_ref,
    wave_ref,
    taps_ref,
    water_ref,
    start_ref,
    length_ref,
    live_ref,
    first_ref,
    twiddle_ref,
    square_ref,
    outer_ref,
    about_ref,
    far_wave_ref,
    far_about_ref,
    stage_ref,
    own_ref,
    part_ref,
    got_ref,
    rows_ref,
    load_sem,
    send_sem,
    recv_sem,
    about_sem,
    part_send_sem,
    part_recv_sem,
):
    sta = lax.axis_index("sta")
    freq = lax.axis_index("freq")
    core = lax.rem(freq, 2)
    chip = freq // 2
    stride = n_sta // (2 * ROUNDS)
    odd = lax.rem(sta // stride, 2)

    def device(steps, index):
        return {"sta": lax.rem(sta + (steps % 4) * stride, n_sta), "freq": index}

    small = [
        pltpu.make_async_copy(source, target, load_sem.at[n])
        for n, (source, target) in enumerate(
            (
                (taps_hbm, taps_ref),
                (water_hbm, water_ref),
                (start_hbm, start_ref),
                (length_hbm, length_ref),
                (live_hbm, live_ref),
            )
        )
    ]
    large = [
        pltpu.make_async_copy(source, target, load_sem.at[5 + n])
        for n, (source, target) in enumerate(
            (
                (wave_hbm, wave_ref),
                (first_hbm, first_ref),
                (twiddle_hbm, twiddle_ref),
                (square_hbm, square_ref),
                (outer_hbm, outer_ref),
            )
        )
    ]
    barrier = pltpu.get_barrier_semaphore()
    for copy in small:
        copy.start()
    for c in range(2):
        pl.semaphore_signal(barrier, inc=1, device_id=device(-1, 2 + c), device_id_type=MESH)
        pl.semaphore_signal(barrier, inc=1, device_id=device(-2, 2 * (1 - chip) + c), device_id_type=MESH)

    group = sta // stride
    pl.semaphore_wait(barrier, 2 + 4 * chip)

    def send(source, slot, target, place, where, order):
        return pltpu.make_async_remote_copy(
            src_ref=source.at[slot],
            dst_ref=target.at[place],
            send_sem=send_sem.at[order],
            recv_sem=(recv_sem if target is far_wave_ref else about_sem).at[place],
            device_id=where,
            device_id_type=MESH,
        )

    def next_sends(source, target, order):
        return [
            send(source, 2 * other + core, target, 0, device(1, 2 * other + core), order + other)
            for other in (1, 0)
        ]

    def second_sends(source, target, order):
        where = device(2, 2 * (1 - chip) + core)
        return [send(source, 2 * n + core, target, 1 + n, where, order + n) for n in range(2)]

    def next_waves():
        return next_sends(wave_hbm, far_wave_ref, 0)

    def next_abouts():
        return next_sends(about_ref, far_about_ref, 2)

    def second_waves():
        return second_sends(wave_hbm, far_wave_ref, 4)

    def second_abouts():
        return second_sends(about_ref, far_about_ref, 6)

    def relay():
        where = device(1, core)
        return [
            send(far_wave_ref, 0, far_wave_ref, 1 + chip, where, 8),
            send(far_about_ref, 0, far_about_ref, 1 + chip, where, 9),
        ]

    def start(copies):
        for copy in copies:
            copy.start()

    relays = group != 3
    feeds_second = (chip == 0) | (group == 2)

    @pl.when((chip == 1) & (group != 2))
    def _():
        start(next_waves())

    @pl.when((chip == 0) & (odd == 0))
    def _():
        start(second_waves())

    for copy in small:
        copy.wait()

    for slot in range(SLOTS):
        about_ref[slot, 0:1, :] = taps_ref[slot : slot + 1, :ROOT]
        about_ref[slot, 1:2, :] = taps_ref[slot : slot + 1, ROOT:]
        about_ref[slot, 2:3, :] = jnp.full((1, ROOT), water_ref[slot] * float(COARSE * ROOT), jnp.float32)
        about_ref[slot, 3:4, :] = jnp.full((1, ROOT), (live_ref[0] > slot).astype(jnp.float32), jnp.float32)
        for s in range(SEG):
            first = start_ref[slot, s]
            after = first + length_ref[slot, s]
            about_ref[slot, 4 + s : 5 + s, :] = jnp.full((1, ROOT), first.astype(jnp.float32), jnp.float32)
            about_ref[slot, 8 + s : 9 + s, :] = jnp.full((1, ROOT), after.astype(jnp.float32), jnp.float32)
        about_ref[slot, 12:16, :] = jnp.zeros((4, ROOT), jnp.float32)

    @pl.when(chip == 1)
    def _():
        start(next_abouts())

    @pl.when(feeds_second)
    def _():
        start(second_abouts())

    for copy in large:
        copy.start()
    for copy in large:
        copy.wait()

    turn = jnp.where((chip == 0) & (group == 1), SLOTS - 1, 0)
    later = feeds_second & jnp.logical_not((chip == 0) & (odd == 0))

    def own_step(slot, carry):
        @pl.when((chip == 1) & (group == 2) & (slot == 2))
        def _():
            start(next_waves())

        @pl.when(later & (slot == turn))
        def _():
            start(second_waves())

        found = spectra(
            wave_ref[slot], about_ref[slot], stage_ref, first_ref[...], twiddle_ref, square_ref
        )
        for s in range(SEG):
            own_ref[slot, s, 0], own_ref[slot, s, 1] = found[s]
        return carry

    lax.fori_loop(0, SLOTS, own_step, 0)

    def slot_of(place):
        return jnp.where(place == 0, freq, core + 2 * (place - 1))

    def share(place, target):
        return pltpu.make_async_remote_copy(
            src_ref=part_ref.at[place, target],
            dst_ref=got_ref.at[jnp.minimum(place, 1), slot_of(place)],
            send_sem=part_send_sem.at[place, target],
            recv_sem=part_recv_sem.at[jnp.minimum(place, 1), slot_of(place)],
            device_id=device(0, target),
            device_id_type=MESH,
        )

    def far_step(place, carry):
        pltpu.make_async_copy(far_wave_ref.at[place], far_wave_ref.at[place], recv_sem.at[place]).wait()
        pltpu.make_async_copy(far_about_ref.at[place], far_about_ref.at[place], about_sem.at[place]).wait()

        @pl.when(relays & (place == 0))
        def _():
            start(relay())

        far = spectra(
            far_wave_ref[place],
            far_about_ref.at[place],
            stage_ref,
            first_ref[...],
            twiddle_ref,
            square_ref,
        )
        pairs = []
        for i in range(SLOTS):
            cross_re = 0.0
            cross_im = 0.0
            for s in range(SEG):
                own_re, own_im = own_ref[i, s, 0], own_ref[i, s, 1]
                far_re, far_im = far[s]
                cross_re = cross_re + own_re * far_re + own_im * far_im
                cross_im = cross_im + own_im * far_re - own_re * far_im
            pairs.append(jnp.concatenate([cross_re, cross_im], axis=1))
        inner = dot(jnp.concatenate(pairs, axis=0).astype(jnp.bfloat16), square_ref[2])
        columns = []
        for i in range(SLOTS):
            inner_re = inner[i * KEPT : (i + 1) * KEPT, :ROOT]
            inner_im = inner[i * KEPT : (i + 1) * KEPT, ROOT:]
            cos_t, sin_t = twiddle_ref[2], twiddle_ref[3]
            columns.append(
                jnp.concatenate(
                    [inner_re * cos_t - inner_im * sin_t, inner_re * sin_t + inner_im * cos_t], axis=0
                ).astype(jnp.bfloat16)
            )
        lagged = dot(outer_ref[...], jnp.concatenate(columns, axis=1))
        for g in range(4):
            band = lagged[g * BAND : (g + 1) * BAND]
            part_ref[place, g] = jnp.concatenate(
                [band[:, i * ROOT : (i + 1) * ROOT] for i in range(SLOTS)], axis=0
            ).astype(jnp.bfloat16)

        @pl.when(place == 0)
        def _():
            for c in range(2):
                share(place, 2 * (1 - chip) + c).start()

        share(place, freq + 1 - 2 * core).start()
        got_ref[jnp.minimum(place, 1), slot_of(place)] = part_ref[place, freq]
        return carry

    lax.fori_loop(0, 3, far_step, 0)

    def arrived(round_index, slot):
        pltpu.make_async_copy(
            got_ref.at[round_index, slot], got_ref.at[round_index, slot], part_recv_sem.at[round_index, slot]
        ).wait()

    for r in range(ROUNDS):
        for slot in [lax.rem(freq + step, 4) for step in range(1, 4)] if r == 0 else [1 - core, 3 - core]:
            arrived(r, slot)

        for j in range(SLOTS):
            piece = got_ref[r, j].astype(jnp.float32)
            for i in range(SLOTS):
                rows_ref[pl.ds(SLOTS * i + j, BAND, stride=SLOTS * SLOTS), :] = piece[i * BAND : (i + 1) * BAND]
        out_ref[r] = rows_ref[...].astype(jnp.bfloat16)

    def finish(copies):
        for copy in copies:
            copy.wait_send()

    for c in range(2):
        share(0, 2 * (1 - chip) + c).wait_send()
    for place in range(3):
        share(place, freq + 1 - 2 * core).wait_send()

    @pl.when(chip == 1)
    def _():
        finish(next_waves() + next_abouts())

    @pl.when(feeds_second)
    def _():
        finish(second_waves() + second_abouts())

    @pl.when(relays)
    def _():
        finish(relay())


def on_device(waveforms, fir_taps, water_level, gap_start, gap_length, live_slots):
    n_sta = lax.axis_size("sta")
    tables = [jnp.asarray(table) for table in make_tables()]

    def pinned(*arrays):
        return [pltpu.with_memory_space_constraint(array, pltpu.HBM) for array in arrays]

    anywhere = pl.BlockSpec(memory_space=pl.ANY)
    rows = BAND * SLOTS * SLOTS
    result = pl.pallas_call(
        functools.partial(kernel, n_sta),
        out_shape=jax.ShapeDtypeStruct((ROUNDS, rows, ROOT), jnp.bfloat16),
        in_specs=[anywhere] * 10,
        out_specs=pl.BlockSpec(memory_space=pltpu.VMEM),
        scratch_shapes=[
            pltpu.VMEM((SLOTS, SEG, COARSE * ROOT), jnp.bfloat16),
            pltpu.VMEM((SLOTS, 2 * ROOT), jnp.float32),
            pltpu.SMEM((SLOTS,), jnp.float32),
            pltpu.SMEM((SLOTS, SEG), jnp.int32),
            pltpu.SMEM((SLOTS, SEG), jnp.int32),
            pltpu.SMEM((1,), jnp.int32),
        ]
        + [pltpu.VMEM(table.shape, table.dtype) for table in tables]
        + [
            pltpu.VMEM((SLOTS, 16, ROOT), jnp.float32),
            pltpu.VMEM((3, SEG, COARSE * ROOT), jnp.bfloat16),
            pltpu.VMEM((3, 16, ROOT), jnp.float32),
            pltpu.VMEM((SEG * COARSE, ROOT), jnp.float32),
            pltpu.VMEM((SLOTS, SEG, 2, KEPT, ROOT), jnp.float32),
            pltpu.VMEM((3, 4, SLOTS * BAND, ROOT), jnp.bfloat16),
            pltpu.VMEM((ROUNDS, SLOTS, SLOTS * BAND, ROOT), jnp.bfloat16),
            pltpu.VMEM((rows, ROOT), jnp.float32),
            pltpu.SemaphoreType.DMA((10,)),
            pltpu.SemaphoreType.DMA((10,)),
            pltpu.SemaphoreType.DMA((3,)),
            pltpu.SemaphoreType.DMA((3,)),
            pltpu.SemaphoreType.DMA((3, 4)),
            pltpu.SemaphoreType.DMA((ROUNDS, SLOTS)),
        ],
        compiler_params=pltpu.CompilerParams(
            collective_id=0, has_side_effects=True, vmem_limit_bytes=40 * 1024 * 1024
        ),
    )(
        *pinned(waveforms, fir_taps, water_level, gap_start, gap_length), live_slots, *pinned(*tables)
    )
    return result.reshape(ROUNDS, BAND, SLOTS, SLOTS, ROOT)


def solution(mesh):
    in_specs = (
        P("sta", None, None),
        P("sta", None),
        P("sta"),
        P("sta", None),
        P("sta", None),
        P("sta"),
    )
    out_specs = P(None, "freq", "sta", None, None)
    return jax.shard_map(
        on_device, mesh=mesh, in_specs=in_specs, out_specs=out_specs, check_vma=False
    )
```

```python
import functools
import math

import jax
import jax.numpy as jnp
import ml_dtypes
import numpy as np
from jax import lax
from jax.experimental import pallas as pl
from jax.experimental.pallas import tpu as pltpu
from jax.sharding import PartitionSpec as P

ROOT = 128
COARSE = 64
LAGROWS = 96
ROUNDS = 2
SLOTS = 4
SEG = 4
KEPT = 72
BAND = LAGROWS // 4
MESH = pl.DeviceIdType.MESH


def as_bf16(table):
    return table.astype(np.float32).astype(ml_dtypes.bfloat16)


def split_bf16(table):
    upper = as_bf16(table)
    return upper, as_bf16(table - upper.astype(np.float64))


def make_tables():
    kept = np.arange(KEPT)
    live = (kept <= 64).astype(np.float64)[:, None]
    full = np.arange(ROOT)
    angle = 2.0 * math.pi / ROOT
    first = kept[:, None] * np.arange(COARSE)[None, :] * angle
    first = np.concatenate([np.cos(first) * live, -np.sin(first) * live], axis=0)
    first_hi, first_lo = split_bf16(first)
    first_table = np.concatenate([first_hi, first_lo], axis=1)
    twist = kept[:, None] * full[None, :] * (angle / ROOT)
    weight = np.where((kept == 0) | (kept == 64), 1.0, 2.0)[:, None] * live
    weight = weight / math.sqrt(SEG * ROOT * ROOT)
    step = np.broadcast_to(kept[:, None] * angle, (KEPT, ROOT))
    twiddles = np.stack(
        [np.cos(twist), np.sin(twist), np.cos(twist) * weight, np.sin(twist) * weight, np.cos(step), np.sin(step)]
    ).astype(np.float32)
    square = full[:, None] * full[None, :] * angle
    cos_b, sin_b = np.cos(square), np.sin(square)
    last = np.block([[cos_b, -sin_b], [sin_b, cos_b]])
    last_hi, last_lo = split_bf16(last)
    inner = as_bf16(np.block([[cos_b, sin_b], [-sin_b, cos_b]]))
    square_tables = np.stack([last_hi, last_lo, inner])
    lag = (np.arange(LAGROWS) - LAGROWS // 2)[:, None] * kept[None, :] * angle
    outer = as_bf16(np.concatenate([np.cos(lag), -np.sin(lag)], axis=1))
    return first_table, twiddles, square_tables, outer


def dot(left, right):
    return jnp.dot(left, right, preferred_element_type=jnp.float32)


def spectra(wave, about, stage, first_table, twiddles, squares):
    place = (
        lax.broadcasted_iota(jnp.int32, (COARSE, ROOT), 0) * ROOT
        + lax.broadcasted_iota(jnp.int32, (COARSE, ROOT), 1)
    ).astype(jnp.float32)
    wide = wave.astype(jnp.float32)
    for row in range(COARSE):
        stage[SEG * row : SEG * (row + 1), :] = wide[:, row * ROOT : (row + 1) * ROOT]
    records = []
    for s in range(SEG):
        start = about[4 + s : 5 + s, :]
        end = about[8 + s : 9 + s, :]
        gone = (place >= start) & (place < end)
        record = jnp.where(gone, 0.0, stage[pl.ds(s, COARSE, stride=SEG), :])
        records.append(record.astype(jnp.bfloat16))
    record = jnp.concatenate(records, axis=1)
    section = dot(first_table, jnp.concatenate([record, record], axis=0))
    cos_t, sin_t = twiddles[0], twiddles[1]
    tap0 = about[0:1, :]
    tap1 = about[1:2, :]
    rows = [(tap0 + tap1 * twiddles[4], -(tap1 * twiddles[5]))]
    for s in range(SEG):
        columns = section[:, s * ROOT : (s + 1) * ROOT]
        rows.append((columns[:KEPT], columns[KEPT:]))
    twisted = jnp.concatenate(
        [
            jnp.concatenate([re * cos_t + im * sin_t, im * cos_t - re * sin_t], axis=1)
            for re, im in rows
        ],
        axis=0,
    )
    upper = twisted.astype(jnp.bfloat16)
    lower = (twisted - upper.astype(jnp.float32)).astype(jnp.bfloat16)
    bins = dot(upper, squares[0]) + dot(lower, squares[0]) + dot(upper, squares[1])
    resp_re, resp_im = bins[:KEPT, :ROOT], bins[:KEPT, ROOT:]
    water = about[2:3, :]
    alive = about[3:4, :]
    found = []
    for s in range(SEG):
        part = bins[(s + 1) * KEPT : (s + 2) * KEPT]
        spec_re, spec_im = part[:, :ROOT], part[:, ROOT:]
        white_re = resp_re * spec_re - resp_im * spec_im
        white_im = resp_re * spec_im + resp_im * spec_re
        factor = alive * lax.rsqrt(white_re * white_re + white_im * white_im + water)
        found.append((white_re * factor, white_im * factor))
    return found


def kernel(
    n_sta,
    wave_hbm,
    taps_hbm,
    water_hbm,
    start_hbm,
    length_hbm,
    live_hbm,
    first_hbm,
    twiddle_hbm,
    square_hbm,
    outer_hbm,
    out_ref,
    wave_ref,
    taps_ref,
    water_ref,
    start_ref,
    length_ref,
    live_ref,
    first_ref,
    twiddle_ref,
    square_ref,
    outer_ref,
    about_ref,
    far_wave_ref,
    far_about_ref,
    stage_ref,
    own_ref,
    part_ref,
    got_ref,
    rows_ref,
    load_sem,
    send_sem,
    recv_sem,
    about_sem,
    part_send_sem,
    part_recv_sem,
):
    sta = lax.axis_index("sta")
    freq = lax.axis_index("freq")
    core = lax.rem(freq, 2)
    chip = freq // 2
    stride = n_sta // (2 * ROUNDS)
    odd = lax.rem(sta // stride, 2)

    def device(steps, index):
        return {"sta": lax.rem(sta + (steps % 4) * stride, n_sta), "freq": index}

    small = [
        pltpu.make_async_copy(source, target, load_sem.at[n])
        for n, (source, target) in enumerate(
            (
                (taps_hbm, taps_ref),
                (water_hbm, water_ref),
                (start_hbm, start_ref),
                (length_hbm, length_ref),
                (live_hbm, live_ref),
            )
        )
    ]
    large = [
        pltpu.make_async_copy(source, target, load_sem.at[5 + n])
        for n, (source, target) in enumerate(
            (
                (wave_hbm, wave_ref),
                (first_hbm, first_ref),
                (twiddle_hbm, twiddle_ref),
                (square_hbm, square_ref),
                (outer_hbm, outer_ref),
            )
        )
    ]
    barrier = pltpu.get_barrier_semaphore()
    for copy in small:
        copy.start()
    for c in range(2):
        pl.semaphore_signal(barrier, inc=1, device_id=device(-1, 2 + c), device_id_type=MESH)
        pl.semaphore_signal(barrier, inc=1, device_id=device(-2, 2 * (1 - chip) + c), device_id_type=MESH)

    group = sta // stride
    pl.semaphore_wait(barrier, 2 + 4 * chip)

    def send(source, slot, target, place, where, order):
        return pltpu.make_async_remote_copy(
            src_ref=source.at[slot],
            dst_ref=target.at[place],
            send_sem=send_sem.at[order],
            recv_sem=(recv_sem if target is far_wave_ref else about_sem).at[place],
            device_id=where,
            device_id_type=MESH,
        )

    def next_sends(source, target, order):
        return [
            send(source, 2 * other + core, target, 0, device(1, 2 * other + core), order + other)
            for other in (1, 0)
        ]

    def second_sends(source, target, order):
        where = device(2, 2 * (1 - chip) + core)
        return [send(source, 2 * n + core, target, 1 + n, where, order + n) for n in range(2)]

    def next_waves():
        return next_sends(wave_hbm, far_wave_ref, 0)

    def next_abouts():
        return next_sends(about_ref, far_about_ref, 2)

    def second_waves():
        return second_sends(wave_hbm, far_wave_ref, 4)

    def second_abouts():
        return second_sends(about_ref, far_about_ref, 6)

    def relay():
        where = device(1, core)
        return [
            send(far_wave_ref, 0, far_wave_ref, 1 + chip, where, 8),
            send(far_about_ref, 0, far_about_ref, 1 + chip, where, 9),
        ]

    def start(copies):
        for copy in copies:
            copy.start()

    relays = group != 3
    feeds_second = (chip == 0) | (group == 2)

    @pl.when((chip == 1) & (group != 2))
    def _():
        start(next_waves())

    @pl.when((chip == 0) & (odd == 0))
    def _():
        start(second_waves())

    for copy in small:
        copy.wait()

    for slot in range(SLOTS):
        about_ref[slot, 0:1, :] = taps_ref[slot : slot + 1, :ROOT]
        about_ref[slot, 1:2, :] = taps_ref[slot : slot + 1, ROOT:]
        about_ref[slot, 2:3, :] = jnp.full((1, ROOT), water_ref[slot] * float(COARSE * ROOT), jnp.float32)
        about_ref[slot, 3:4, :] = jnp.full((1, ROOT), (live_ref[0] > slot).astype(jnp.float32), jnp.float32)
        for s in range(SEG):
            first = start_ref[slot, s]
            after = first + length_ref[slot, s]
            about_ref[slot, 4 + s : 5 + s, :] = jnp.full((1, ROOT), first.astype(jnp.float32), jnp.float32)
            about_ref[slot, 8 + s : 9 + s, :] = jnp.full((1, ROOT), after.astype(jnp.float32), jnp.float32)
        about_ref[slot, 12:16, :] = jnp.zeros((4, ROOT), jnp.float32)

    @pl.when(chip == 1)
    def _():
        start(next_abouts())

    @pl.when(feeds_second)
    def _():
        start(second_abouts())

    for copy in large:
        copy.start()
    for copy in large:
        copy.wait()

    turn = jnp.where((chip == 0) & (group == 1), SLOTS - 1, 0)
    later = feeds_second & jnp.logical_not((chip == 0) & (odd == 0))

    def own_step(slot, carry):
        @pl.when((chip == 1) & (group == 2) & (slot == 2))
        def _():
            start(next_waves())

        @pl.when(later & (slot == turn))
        def _():
            start(second_waves())

        found = spectra(
            wave_ref[slot], about_ref[slot], stage_ref, first_ref[...], twiddle_ref, square_ref
        )
        for s in range(SEG):
            own_ref[slot, s, 0], own_ref[slot, s, 1] = found[s]
        return carry

    lax.fori_loop(0, SLOTS, own_step, 0)

    def slot_of(place):
        return jnp.where(place == 0, freq, core + 2 * (place - 1))

    def share(place, target):
        return pltpu.make_async_remote_copy(
            src_ref=part_ref.at[place, target],
            dst_ref=got_ref.at[jnp.minimum(place, 1), slot_of(place)],
            send_sem=part_send_sem.at[place, target],
            recv_sem=part_recv_sem.at[jnp.minimum(place, 1), slot_of(place)],
            device_id=device(0, target),
            device_id_type=MESH,
        )

    def lay(round_index, slot, block):
        piece = block.astype(jnp.float32)
        for i in range(SLOTS):
            rows_ref[round_index, pl.ds(SLOTS * i + slot, BAND, stride=SLOTS * SLOTS), :] = piece[
                i * BAND : (i + 1) * BAND
            ]

    def far_step(place, carry):
        pltpu.make_async_copy(far_wave_ref.at[place], far_wave_ref.at[place], recv_sem.at[place]).wait()
        pltpu.make_async_copy(far_about_ref.at[place], far_about_ref.at[place], about_sem.at[place]).wait()

        @pl.when(relays & (place == 0))
        def _():
            start(relay())

        far = spectra(
            far_wave_ref[place],
            far_about_ref.at[place],
            stage_ref,
            first_ref[...],
            twiddle_ref,
            square_ref,
        )
        pairs = []
        for i in range(SLOTS):
            cross_re = 0.0
            cross_im = 0.0
            for s in range(SEG):
                own_re, own_im = own_ref[i, s, 0], own_ref[i, s, 1]
                far_re, far_im = far[s]
                cross_re = cross_re + own_re * far_re + own_im * far_im
                cross_im = cross_im + own_im * far_re - own_re * far_im
            pairs.append(jnp.concatenate([cross_re, cross_im], axis=1))
        inner = dot(jnp.concatenate(pairs, axis=0).astype(jnp.bfloat16), square_ref[2])
        columns = []
        for i in range(SLOTS):
            inner_re = inner[i * KEPT : (i + 1) * KEPT, :ROOT]
            inner_im = inner[i * KEPT : (i + 1) * KEPT, ROOT:]
            cos_t, sin_t = twiddle_ref[2], twiddle_ref[3]
            columns.append(
                jnp.concatenate(
                    [inner_re * cos_t - inner_im * sin_t, inner_re * sin_t + inner_im * cos_t], axis=0
                ).astype(jnp.bfloat16)
            )
        lagged = dot(outer_ref[...], jnp.concatenate(columns, axis=1))
        for g in range(4):
            band = lagged[g * BAND : (g + 1) * BAND]
            part_ref[place, g] = jnp.concatenate(
                [band[:, i * ROOT : (i + 1) * ROOT] for i in range(SLOTS)], axis=0
            ).astype(jnp.bfloat16)

        @pl.when(place == 0)
        def _():
            for c in range(2):
                share(place, 2 * (1 - chip) + c).start()

        share(place, freq + 1 - 2 * core).start()
        lay(jnp.minimum(place, 1), slot_of(place), part_ref[place, freq])
        return carry

    lax.fori_loop(0, 3, far_step, 0)

    def arrived(round_index, slot):
        pltpu.make_async_copy(
            got_ref.at[round_index, slot], got_ref.at[round_index, slot], part_recv_sem.at[round_index, slot]
        ).wait()

    for r in range(ROUNDS):
        others = [freq + 1 - 2 * core, 2 * (1 - chip), 2 * (1 - chip) + 1] if r == 0 else [1 - core, 3 - core]
        for slot in others:
            arrived(r, slot)
            lay(r, slot, got_ref[r, slot])
        out_ref[r] = rows_ref[r].astype(jnp.bfloat16)

    def finish(copies):
        for copy in copies:
            copy.wait_send()

    for c in range(2):
        share(0, 2 * (1 - chip) + c).wait_send()
    for place in range(3):
        share(place, freq + 1 - 2 * core).wait_send()

    @pl.when(chip == 1)
    def _():
        finish(next_waves() + next_abouts())

    @pl.when(feeds_second)
    def _():
        finish(second_waves() + second_abouts())

    @pl.when(relays)
    def _():
        finish(relay())


def on_device(waveforms, fir_taps, water_level, gap_start, gap_length, live_slots):
    n_sta = lax.axis_size("sta")
    tables = [jnp.asarray(table) for table in make_tables()]

    def pinned(*arrays):
        return [pltpu.with_memory_space_constraint(array, pltpu.HBM) for array in arrays]

    anywhere = pl.BlockSpec(memory_space=pl.ANY)
    rows = BAND * SLOTS * SLOTS
    result = pl.pallas_call(
        functools.partial(kernel, n_sta),
        out_shape=jax.ShapeDtypeStruct((ROUNDS, rows, ROOT), jnp.bfloat16),
        in_specs=[anywhere] * 10,
        out_specs=pl.BlockSpec(memory_space=pltpu.VMEM),
        scratch_shapes=[
            pltpu.VMEM((SLOTS, SEG, COARSE * ROOT), jnp.bfloat16),
            pltpu.VMEM((SLOTS, 2 * ROOT), jnp.float32),
            pltpu.SMEM((SLOTS,), jnp.float32),
            pltpu.SMEM((SLOTS, SEG), jnp.int32),
            pltpu.SMEM((SLOTS, SEG), jnp.int32),
            pltpu.SMEM((1,), jnp.int32),
        ]
        + [pltpu.VMEM(table.shape, table.dtype) for table in tables]
        + [
            pltpu.VMEM((SLOTS, 16, ROOT), jnp.float32),
            pltpu.VMEM((3, SEG, COARSE * ROOT), jnp.bfloat16),
            pltpu.VMEM((3, 16, ROOT), jnp.float32),
            pltpu.VMEM((SEG * COARSE, ROOT), jnp.float32),
            pltpu.VMEM((SLOTS, SEG, 2, KEPT, ROOT), jnp.float32),
            pltpu.VMEM((3, 4, SLOTS * BAND, ROOT), jnp.bfloat16),
            pltpu.VMEM((ROUNDS, SLOTS, SLOTS * BAND, ROOT), jnp.bfloat16),
            pltpu.VMEM((ROUNDS, rows, ROOT), jnp.float32),
            pltpu.SemaphoreType.DMA((10,)),
            pltpu.SemaphoreType.DMA((10,)),
            pltpu.SemaphoreType.DMA((3,)),
            pltpu.SemaphoreType.DMA((3,)),
            pltpu.SemaphoreType.DMA((3, 4)),
            pltpu.SemaphoreType.DMA((ROUNDS, SLOTS)),
        ],
        compiler_params=pltpu.CompilerParams(
            collective_id=0, has_side_effects=True, vmem_limit_bytes=40 * 1024 * 1024
        ),
    )(
        *pinned(waveforms, fir_taps, water_level, gap_start, gap_length), live_slots, *pinned(*tables)
    )
    return result.reshape(ROUNDS, BAND, SLOTS, SLOTS, ROOT)


def solution(mesh):
    in_specs = (
        P("sta", None, None),
        P("sta", None),
        P("sta"),
        P("sta", None),
        P("sta", None),
        P("sta"),
    )
    out_specs = P(None, "freq", "sta", None, None)
    return jax.shard_map(
        on_device, mesh=mesh, in_specs=in_specs, out_specs=out_specs, check_vma=False
    )
```

```python
import functools
import math

import jax
import jax.numpy as jnp
import ml_dtypes
import numpy as np
from jax import lax
from jax.experimental import pallas as pl
from jax.experimental.pallas import tpu as pltpu
from jax.sharding import PartitionSpec as P

ROOT = 128
COARSE = 64
LAGROWS = 96
ROUNDS = 2
SLOTS = 4
SEG = 4
KEPT = 72
BAND = LAGROWS // 4
MESH = pl.DeviceIdType.MESH


def as_bf16(table):
    return table.astype(np.float32).astype(ml_dtypes.bfloat16)


def split_bf16(table):
    upper = as_bf16(table)
    return upper, as_bf16(table - upper.astype(np.float64))


def make_tables():
    kept = np.arange(KEPT)
    live = (kept <= 64).astype(np.float64)[:, None]
    full = np.arange(ROOT)
    angle = 2.0 * math.pi / ROOT
    first = kept[:, None] * np.arange(COARSE)[None, :] * angle
    first = np.concatenate([np.cos(first) * live, -np.sin(first) * live], axis=0)
    first_hi, first_lo = split_bf16(first)
    first_table = np.concatenate([first_hi, first_lo], axis=1)
    twist = kept[:, None] * full[None, :] * (angle / ROOT)
    weight = np.where((kept == 0) | (kept == 64), 1.0, 2.0)[:, None] * live
    weight = weight / math.sqrt(SEG * ROOT * ROOT)
    step = np.broadcast_to(kept[:, None] * angle, (KEPT, ROOT))
    twiddles = np.stack(
        [np.cos(twist), np.sin(twist), np.cos(twist) * weight, np.sin(twist) * weight, np.cos(step), np.sin(step)]
    ).astype(np.float32)
    square = full[:, None] * full[None, :] * angle
    cos_b, sin_b = np.cos(square), np.sin(square)
    last = np.block([[cos_b, -sin_b], [sin_b, cos_b]])
    last_hi, last_lo = split_bf16(last)
    inner = as_bf16(np.block([[cos_b, sin_b], [-sin_b, cos_b]]))
    square_tables = np.stack([last_hi, last_lo, inner])
    lag = (np.arange(LAGROWS) - LAGROWS // 2)[:, None] * kept[None, :] * angle
    outer = as_bf16(np.concatenate([np.cos(lag), -np.sin(lag)], axis=1))
    return first_table, twiddles, square_tables, outer


def dot(left, right):
    return jnp.dot(left, right, preferred_element_type=jnp.float32)


def spectra(wave, about, stage, first_table, twiddles, squares):
    place = (
        lax.broadcasted_iota(jnp.int32, (COARSE, ROOT), 0) * ROOT
        + lax.broadcasted_iota(jnp.int32, (COARSE, ROOT), 1)
    ).astype(jnp.float32)
    wide = wave.astype(jnp.float32)
    for row in range(COARSE):
        stage[SEG * row : SEG * (row + 1), :] = wide[:, row * ROOT : (row + 1) * ROOT]
    records = []
    for s in range(SEG):
        start = about[4 + s : 5 + s, :]
        end = about[8 + s : 9 + s, :]
        gone = (place >= start) & (place < end)
        record = jnp.where(gone, 0.0, stage[pl.ds(s, COARSE, stride=SEG), :])
        records.append(record.astype(jnp.bfloat16))
    record = jnp.concatenate(records, axis=1)
    section = dot(first_table, jnp.concatenate([record, record], axis=0))
    cos_t, sin_t = twiddles[0], twiddles[1]
    tap0 = about[0:1, :]
    tap1 = about[1:2, :]
    rows = [(tap0 + tap1 * twiddles[4], -(tap1 * twiddles[5]))]
    for s in range(SEG):
        columns = section[:, s * ROOT : (s + 1) * ROOT]
        rows.append((columns[:KEPT], columns[KEPT:]))
    twisted = jnp.concatenate(
        [
            jnp.concatenate([re * cos_t + im * sin_t, im * cos_t - re * sin_t], axis=1)
            for re, im in rows
        ],
        axis=0,
    )
    upper = twisted.astype(jnp.bfloat16)
    lower = (twisted - upper.astype(jnp.float32)).astype(jnp.bfloat16)
    bins = dot(upper, squares[0]) + dot(lower, squares[0]) + dot(upper, squares[1])
    resp_re, resp_im = bins[:KEPT, :ROOT], bins[:KEPT, ROOT:]
    water = about[2:3, :]
    alive = about[3:4, :]
    found = []
    for s in range(SEG):
        part = bins[(s + 1) * KEPT : (s + 2) * KEPT]
        spec_re, spec_im = part[:, :ROOT], part[:, ROOT:]
        white_re = resp_re * spec_re - resp_im * spec_im
        white_im = resp_re * spec_im + resp_im * spec_re
        factor = alive * lax.rsqrt(white_re * white_re + white_im * white_im + water)
        found.append((white_re * factor, white_im * factor))
    return found


def kernel(
    n_sta,
    wave_hbm,
    taps_hbm,
    water_hbm,
    start_hbm,
    length_hbm,
    live_hbm,
    first_hbm,
    twiddle_hbm,
    square_hbm,
    outer_hbm,
    out_ref,
    wave_ref,
    taps_ref,
    water_ref,
    start_ref,
    length_ref,
    live_ref,
    first_ref,
    twiddle_ref,
    square_ref,
    outer_ref,
    about_ref,
    far_wave_ref,
    far_about_ref,
    stage_ref,
    own_ref,
    part_ref,
    got_ref,
    rows_ref,
    load_sem,
    send_sem,
    recv_sem,
    about_sem,
    part_send_sem,
    part_recv_sem,
):
    sta = lax.axis_index("sta")
    freq = lax.axis_index("freq")
    core = lax.rem(freq, 2)
    chip = freq // 2
    stride = n_sta // (2 * ROUNDS)
    odd = lax.rem(sta // stride, 2)

    def device(steps, index):
        return {"sta": lax.rem(sta + (steps % 4) * stride, n_sta), "freq": index}

    small = [
        pltpu.make_async_copy(source, target, load_sem.at[n])
        for n, (source, target) in enumerate(
            (
                (taps_hbm, taps_ref),
                (water_hbm, water_ref),
                (start_hbm, start_ref),
                (length_hbm, length_ref),
                (live_hbm, live_ref),
            )
        )
    ]
    large = [
        pltpu.make_async_copy(source, target, load_sem.at[5 + n])
        for n, (source, target) in enumerate(
            (
                (wave_hbm, wave_ref),
                (first_hbm, first_ref),
                (twiddle_hbm, twiddle_ref),
                (square_hbm, square_ref),
                (outer_hbm, outer_ref),
            )
        )
    ]
    barrier = pltpu.get_barrier_semaphore()
    for copy in small:
        copy.start()
    for c in range(2):
        pl.semaphore_signal(barrier, inc=1, device_id=device(-1, 2 + c), device_id_type=MESH)
        pl.semaphore_signal(barrier, inc=1, device_id=device(-2, 2 * (1 - chip) + c), device_id_type=MESH)

    group = sta // stride
    pl.semaphore_wait(barrier, 2 + 4 * chip)

    def send(source, slot, target, place, where, order):
        return pltpu.make_async_remote_copy(
            src_ref=source.at[slot],
            dst_ref=target.at[place],
            send_sem=send_sem.at[order],
            recv_sem=(recv_sem if target is far_wave_ref else about_sem).at[place],
            device_id=where,
            device_id_type=MESH,
        )

    def next_sends(source, target, order):
        return [
            send(source, 2 * other + core, target, 0, device(1, 2 * other + core), order + other)
            for other in (1, 0)
        ]

    def second_sends(source, target, order):
        where = device(2, 2 * (1 - chip) + core)
        return [send(source, 2 * n + core, target, 1 + n, where, order + n) for n in range(2)]

    def next_waves():
        return next_sends(wave_hbm, far_wave_ref, 0)

    def next_abouts():
        return next_sends(about_ref, far_about_ref, 2)

    def second_waves():
        return second_sends(wave_hbm, far_wave_ref, 4)

    def second_abouts():
        return second_sends(about_ref, far_about_ref, 6)

    def relay():
        where = device(1, core)
        return [
            send(far_wave_ref, 0, far_wave_ref, 1 + chip, where, 8),
            send(far_about_ref, 0, far_about_ref, 1 + chip, where, 9),
        ]

    def start(copies):
        for copy in copies:
            copy.start()

    relays = group != 3
    feeds_second = (chip == 0) | (group == 2)

    @pl.when((chip == 1) & (group != 2))
    def _():
        start(next_waves())

    @pl.when((chip == 0) & (odd == 0))
    def _():
        start(second_waves())

    for copy in small:
        copy.wait()

    for slot in range(SLOTS):
        about_ref[slot, 0:1, :] = taps_ref[slot : slot + 1, :ROOT]
        about_ref[slot, 1:2, :] = taps_ref[slot : slot + 1, ROOT:]
        about_ref[slot, 2:3, :] = jnp.full((1, ROOT), water_ref[slot] * float(COARSE * ROOT), jnp.float32)
        about_ref[slot, 3:4, :] = jnp.full((1, ROOT), (live_ref[0] > slot).astype(jnp.float32), jnp.float32)
        for s in range(SEG):
            first = start_ref[slot, s]
            after = first + length_ref[slot, s]
            about_ref[slot, 4 + s : 5 + s, :] = jnp.full((1, ROOT), first.astype(jnp.float32), jnp.float32)
            about_ref[slot, 8 + s : 9 + s, :] = jnp.full((1, ROOT), after.astype(jnp.float32), jnp.float32)
        about_ref[slot, 12:16, :] = jnp.zeros((4, ROOT), jnp.float32)

    @pl.when(chip == 1)
    def _():
        start(next_abouts())

    @pl.when(feeds_second)
    def _():
        start(second_abouts())

    for copy in large:
        copy.start()
    for copy in large:
        copy.wait()

    turn = jnp.where((chip == 0) & (group == 1), SLOTS - 1, 0)
    later = feeds_second & jnp.logical_not((chip == 0) & (odd == 0))

    def own_step(slot, carry):
        @pl.when((chip == 1) & (group == 2) & (slot == 2))
        def _():
            start(next_waves())

        @pl.when(later & (slot == turn))
        def _():
            start(second_waves())

        found = spectra(
            wave_ref[slot], about_ref[slot], stage_ref, first_ref[...], twiddle_ref, square_ref
        )
        for s in range(SEG):
            own_ref[slot, s, 0], own_ref[slot, s, 1] = found[s]
        return carry

    lax.fori_loop(0, SLOTS, own_step, 0)

    def slot_of(place):
        return jnp.where(place == 0, freq, core + 2 * (place - 1))

    def share(place, target):
        return pltpu.make_async_remote_copy(
            src_ref=part_ref.at[place, target],
            dst_ref=got_ref.at[jnp.minimum(place, 1), slot_of(place)],
            send_sem=part_send_sem.at[place, target],
            recv_sem=part_recv_sem.at[jnp.minimum(place, 1), slot_of(place)],
            device_id=device(0, target),
            device_id_type=MESH,
        )

    def lay(round_index, slot, block):
        piece = block.astype(jnp.float32)
        for i in range(SLOTS):
            rows_ref[round_index, pl.ds(SLOTS * i + slot, BAND, stride=SLOTS * SLOTS), :] = piece[
                i * BAND : (i + 1) * BAND
            ]

    def far_step(place, carry):
        pltpu.make_async_copy(far_wave_ref.at[place], far_wave_ref.at[place], recv_sem.at[place]).wait()
        pltpu.make_async_copy(far_about_ref.at[place], far_about_ref.at[place], about_sem.at[place]).wait()

        @pl.when(relays & (place == 0))
        def _():
            start(relay())

        far = spectra(
            far_wave_ref[place],
            far_about_ref.at[place],
            stage_ref,
            first_ref[...],
            twiddle_ref,
            square_ref,
        )
        pairs = []
        for i in range(SLOTS):
            cross_re = 0.0
            cross_im = 0.0
            for s in range(SEG):
                own_re, own_im = own_ref[i, s, 0], own_ref[i, s, 1]
                far_re, far_im = far[s]
                cross_re = cross_re + own_re * far_re + own_im * far_im
                cross_im = cross_im + own_im * far_re - own_re * far_im
            pairs.append(jnp.concatenate([cross_re, cross_im], axis=1))
        inner = dot(jnp.concatenate(pairs, axis=0).astype(jnp.bfloat16), square_ref[2])
        columns = []
        for i in range(SLOTS):
            inner_re = inner[i * KEPT : (i + 1) * KEPT, :ROOT]
            inner_im = inner[i * KEPT : (i + 1) * KEPT, ROOT:]
            cos_t, sin_t = twiddle_ref[2], twiddle_ref[3]
            columns.append(
                jnp.concatenate(
                    [inner_re * cos_t - inner_im * sin_t, inner_re * sin_t + inner_im * cos_t], axis=0
                ).astype(jnp.bfloat16)
            )
        lagged = dot(outer_ref[...], jnp.concatenate(columns, axis=1))
        def keep(g):
            band = lagged[g * BAND : (g + 1) * BAND]
            part_ref[place, g] = jnp.concatenate(
                [band[:, i * ROOT : (i + 1) * ROOT] for i in range(SLOTS)], axis=0
            ).astype(jnp.bfloat16)

        for half in range(2):

            @pl.when((place == 0) | (chip == half))
            def _(half=half):
                keep(2 * half)
                keep(2 * half + 1)

        @pl.when(place == 0)
        def _():
            for c in range(2):
                share(place, 2 * (1 - chip) + c).start()

        share(place, freq + 1 - 2 * core).start()
        lay(jnp.minimum(place, 1), slot_of(place), part_ref[place, freq])
        return carry

    lax.fori_loop(0, 3, far_step, 0)

    def arrived(round_index, slot):
        pltpu.make_async_copy(
            got_ref.at[round_index, slot], got_ref.at[round_index, slot], part_recv_sem.at[round_index, slot]
        ).wait()

    for r in range(ROUNDS):
        others = [freq + 1 - 2 * core, 2 * (1 - chip), 2 * (1 - chip) + 1] if r == 0 else [1 - core, 3 - core]
        for slot in others:
            arrived(r, slot)
            lay(r, slot, got_ref[r, slot])
        out_ref[r] = rows_ref[r].astype(jnp.bfloat16)

    def finish(copies):
        for copy in copies:
            copy.wait_send()

    for c in range(2):
        share(0, 2 * (1 - chip) + c).wait_send()
    for place in range(3):
        share(place, freq + 1 - 2 * core).wait_send()

    @pl.when(chip == 1)
    def _():
        finish(next_waves() + next_abouts())

    @pl.when(feeds_second)
    def _():
        finish(second_waves() + second_abouts())

    @pl.when(relays)
    def _():
        finish(relay())


def on_device(waveforms, fir_taps, water_level, gap_start, gap_length, live_slots):
    n_sta = lax.axis_size("sta")
    tables = [jnp.asarray(table) for table in make_tables()]

    def pinned(*arrays):
        return [pltpu.with_memory_space_constraint(array, pltpu.HBM) for array in arrays]

    anywhere = pl.BlockSpec(memory_space=pl.ANY)
    rows = BAND * SLOTS * SLOTS
    result = pl.pallas_call(
        functools.partial(kernel, n_sta),
        out_shape=jax.ShapeDtypeStruct((ROUNDS, rows, ROOT), jnp.bfloat16),
        in_specs=[anywhere] * 10,
        out_specs=pl.BlockSpec(memory_space=pltpu.VMEM),
        scratch_shapes=[
            pltpu.VMEM((SLOTS, SEG, COARSE * ROOT), jnp.bfloat16),
            pltpu.VMEM((SLOTS, 2 * ROOT), jnp.float32),
            pltpu.SMEM((SLOTS,), jnp.float32),
            pltpu.SMEM((SLOTS, SEG), jnp.int32),
            pltpu.SMEM((SLOTS, SEG), jnp.int32),
            pltpu.SMEM((1,), jnp.int32),
        ]
        + [pltpu.VMEM(table.shape, table.dtype) for table in tables]
        + [
            pltpu.VMEM((SLOTS, 16, ROOT), jnp.float32),
            pltpu.VMEM((3, SEG, COARSE * ROOT), jnp.bfloat16),
            pltpu.VMEM((3, 16, ROOT), jnp.float32),
            pltpu.VMEM((SEG * COARSE, ROOT), jnp.float32),
            pltpu.VMEM((SLOTS, SEG, 2, KEPT, ROOT), jnp.float32),
            pltpu.VMEM((3, 4, SLOTS * BAND, ROOT), jnp.bfloat16),
            pltpu.VMEM((ROUNDS, SLOTS, SLOTS * BAND, ROOT), jnp.bfloat16),
            pltpu.VMEM((ROUNDS, rows, ROOT), jnp.float32),
            pltpu.SemaphoreType.DMA((10,)),
            pltpu.SemaphoreType.DMA((10,)),
            pltpu.SemaphoreType.DMA((3,)),
            pltpu.SemaphoreType.DMA((3,)),
            pltpu.SemaphoreType.DMA((3, 4)),
            pltpu.SemaphoreType.DMA((ROUNDS, SLOTS)),
        ],
        compiler_params=pltpu.CompilerParams(
            collective_id=0, has_side_effects=True, vmem_limit_bytes=40 * 1024 * 1024
        ),
    )(
        *pinned(waveforms, fir_taps, water_level, gap_start, gap_length), live_slots, *pinned(*tables)
    )
    return result.reshape(ROUNDS, BAND, SLOTS, SLOTS, ROOT)


def solution(mesh):
    in_specs = (
        P("sta", None, None),
        P("sta", None),
        P("sta"),
        P("sta", None),
        P("sta", None),
        P("sta"),
    )
    out_specs = P(None, "freq", "sta", None, None)
    return jax.shard_map(
        on_device, mesh=mesh, in_specs=in_specs, out_specs=out_specs, check_vma=False
    )
```
